128 devices in a mesh: leaf: 16 (over y, z), row: 8 (over x, core).
Axes of the slice: x: 4, y: 4, z: 4, core: 2. Of those that a mesh axis runs over, the one named last changes fastest.
Arguments:
- panel0: float32 [24576, 512], P(('leaf', 'row')), may hold values from -3 to 30, as said below
- panel1: float32 [12288, 512], P(('leaf', 'row')), may hold values from -3 to 30
- panel2: float32 [6144, 512], P(('leaf', 'row')), may hold values from -3 to 30
- panel3: float32 [3072, 512], P(('leaf', 'row')), may hold values from -3 to 30
- maps1: int32 [16, 8], replicated, may hold values from 0 to 11, as said below
- maps2: int32 [8, 8], replicated, may hold values from 0 to 11, as said below
- maps3: int32 [4, 8], replicated, may hold values from 0 to 11, as said below
Outputs:
- update_top: float32 [2048, 1024], P(('leaf', 'row'))
The draws below stay inside these ranges and needn't reach their ends.
Inputs may be any that keep to these rules, and one draw needn't show every extreme that they name: `panel0`: each front's first 512 rows form a symmetric matrix, and every assembled pivot block is positive definite. `maps1`: each row lists distinct parent block numbers. `maps2`: each row lists distinct parent block numbers. `maps3`: each row lists distinct parent block numbers.
All inputs are finite; a program needn't handle non-finite values.
Results may differ from the reference program's by a relative error of at most 0.0003.
Values sent between devices are 32-bit elements; how exact they have to be, the bound alone decides.
No kernel may reach another device: no remote copies, remote signals or barrier semaphores. Data moves between devices by JAX's collectives and lax.ppermute only.
A program may use at most 128 MiB of HBM per device.

```python
import math
import jax
import jax.numpy as jnp
from jax import lax

BLOCK = 128
PIV = 512
UPD = 1024
N_LEAF = 16


def draw_noise(key, shape):
    return jnp.clip(jax.random.normal(key, shape, jnp.float32), -4.0, 4.0)


def make_panels(key, front_count):
    keys = jax.random.split(key, 3)
    diagonal = jax.random.uniform(keys[0], (front_count, PIV), jnp.float32, 12.0, 24.0)
    raw = draw_noise(keys[1], (front_count, PIV, PIV)) * (3.6 / math.sqrt(PIV))
    pivot = (raw + jnp.swapaxes(raw, 1, 2)) / math.sqrt(2.0)
    pivot = pivot + diagonal[:, :, None] * jnp.eye(PIV, dtype=jnp.float32)[None, :, :]
    coupling = draw_noise(keys[2], (front_count, UPD, PIV)) * (3.0 / math.sqrt(PIV))
    stacked = jnp.concatenate([pivot, coupling], axis=1)
    return stacked.reshape(front_count * (PIV + UPD), PIV)


def make_maps(key, child_count):
    keys = jax.random.split(key, child_count)
    parent_blocks = (PIV + UPD) // BLOCK

    def one_row(one_key):
        return jax.random.permutation(one_key, parent_blocks)[:UPD // BLOCK]
    return jax.vmap(one_row)(keys).astype(jnp.int32)


def draw_panel0(key, part):
    return make_panels(jax.random.fold_in(key, 10), N_LEAF)


def draw_panel1(key, part):
    return make_panels(jax.random.fold_in(key, 11), N_LEAF // 2)


def draw_panel2(key, part):
    return make_panels(jax.random.fold_in(key, 12), N_LEAF // 4)


def draw_panel3(key, part):
    return make_panels(jax.random.fold_in(key, 13), N_LEAF // 8)


def draw_maps1(key, part):
    return make_maps(jax.random.fold_in(key, 21), N_LEAF)


def draw_maps2(key, part):
    return make_maps(jax.random.fold_in(key, 22), N_LEAF // 2)


def draw_maps3(key, part):
    return make_maps(jax.random.fold_in(key, 23), N_LEAF // 4)


def setup_inputs(seed: int = 0) -> dict:
    splits = jax.random.split(jax.random.key(seed), 8)
    panel0 = draw_panel0(jax.random.fold_in(splits[7], 71), 0)
    panel1 = draw_panel1(jax.random.fold_in(splits[7], 71), 0)
    panel2 = draw_panel2(jax.random.fold_in(splits[7], 71), 0)
    panel3 = draw_panel3(jax.random.fold_in(splits[7], 71), 0)
    maps1 = draw_maps1(jax.random.fold_in(splits[7], 71), 0)
    maps2 = draw_maps2(jax.random.fold_in(splits[7], 71), 0)
    maps3 = draw_maps3(jax.random.fold_in(splits[7], 71), 0)
    return {"panel0": panel0, "panel1": panel1, "panel2": panel2, "panel3": panel3, "maps1": maps1, "maps2": maps2, "maps3": maps3}


exact_mode = lax.Precision.HIGHEST

def extend_add(update, blocks):
    parent_blocks = (PIV + UPD) // BLOCK
    child_blocks = blocks.shape[0]
    onehot = (blocks[:, None] == jnp.arange(parent_blocks, dtype=jnp.int32)[None, :]).astype(jnp.float32)
    tile_grid = update.reshape(child_blocks, BLOCK, child_blocks, BLOCK)
    spread = jnp.einsum('ia,ixjy->axjy', onehot, tile_grid, precision=exact_mode)
    placed = jnp.einsum('axjy,jb->axby', spread, onehot, precision=exact_mode)
    return placed.reshape(parent_blocks * BLOCK, parent_blocks * BLOCK)

def factor_front(front_rows, trailing, upper_panel):
    assembled = front_rows + upper_panel
    factor = jnp.linalg.cholesky(assembled[:PIV])
    columns = lax.linalg.triangular_solve(factor, assembled[PIV:], left_side=False, lower=True, transpose_a=True)
    return trailing - jnp.dot(columns.astype(jnp.float32), columns.T.astype(jnp.float32), precision=exact_mode, preferred_element_type=jnp.float32)

def reference(panel0, panel1, panel2, panel3, maps1, maps2, maps3):
    front_size = PIV + UPD
    child_blocks = UPD // BLOCK
    fronts = panel0.reshape(N_LEAF, front_size, PIV)

    def leaf_front(front_rows):
        return factor_front(front_rows, jnp.zeros((UPD, UPD), jnp.float32), jnp.zeros((front_size, PIV), jnp.float32))
    schur = lax.map(leaf_front, fronts)
    level_index = 1
    for panel_rows, block_maps in ((panel1, maps1), (panel2, maps2), (panel3, maps3)):
        front_count = N_LEAF // 2 ** level_index
        fronts = panel_rows.reshape(front_count, front_size, PIV)
        children = schur.reshape(front_count, 2, UPD, UPD)
        map_pairs = block_maps.reshape(front_count, 2, child_blocks)

        def parent(inputs):
            front_rows, child_pair, map_pair = inputs
            upper = extend_add(child_pair[0], map_pair[0]) + extend_add(child_pair[1], map_pair[1])
            return factor_front(front_rows, upper[PIV:, PIV:], upper[:, :PIV])
        schur = lax.map(parent, (fronts, children, map_pairs))
        level_index = level_index + 1
    return schur.reshape(N_LEAF // 8 * UPD, UPD)
```

```python
import functools

import jax
import jax.numpy as jnp
from jax import lax
from jax.experimental import pallas as pl
from jax.experimental.pallas import tpu as pltpu
from jax.sharding import PartitionSpec as P

BLOCK = 128
PIV = 512
UPD = 1024
FRONT = PIV + UPD
SUB = 8
WIDTH = 16
PIV_BLOCKS = PIV // BLOCK
UPD_BLOCKS = UPD // BLOCK
PIECE_ROWS = 192
LOWER = [(p, q) for p in range(PIV_BLOCKS) for q in range(p + 1)]
PACKED = [(a, b) for a in range(UPD_BLOCKS) for b in range(a + 1)]
HALF_ROWS = len(LOWER) * BLOCK // 2
SHARE_ROWS = len(PACKED) * BLOCK // 8
VMEM_BYTES = 56 * 1024 * 1024

f32 = jnp.float32
bf16 = jnp.bfloat16


def split(x):
    high = x.astype(bf16)
    return high, (x - high.astype(f32)).astype(bf16)


def dot3(left, right, transposed=False):
    dims = (((1,), (1 if transposed else 0,)), ((), ()))
    dot = functools.partial(lax.dot_general, dimension_numbers=dims, preferred_element_type=f32)
    return dot(left[0], right[0]) + (dot(left[0], right[1]) + dot(left[1], right[0]))


def reciprocal(x):
    r = pltpu.reciprocal(x, approx=True)
    return r * (2.0 - x * r)


def inverse_block(rows):
    count = len(rows)
    parts = WIDTH // SUB
    shape = (SUB, BLOCK)
    lane = lax.broadcasted_iota(jnp.int32, shape, 1)
    sub = lax.broadcasted_iota(jnp.int32, shape, 0)
    rows = list(rows)

    def row_of(x, t):
        return jnp.broadcast_to(x[t : t + 1, :], shape)

    def lane_of(x, l):
        return jnp.broadcast_to(x[:, l : l + 1], shape)

    for g in range(count // parts):
        base = g * WIDTH
        inside = (lane >= base) & (lane < base + WIDTH)
        cols = [[lane_of(rows[parts * g + h], base + i) for i in range(WIDTH)] for h in range(parts)]
        strip = [
            jnp.where(inside, jnp.where(lane == base + h * SUB + sub, 1.0, 0.0), rows[parts * g + h])
            for h in range(parts)
        ]
        for i in range(0, WIDTH, 2):
            h, t = i // SUB, i % SUB
            a, b = row_of(cols[h][i], t), row_of(cols[h][i + 1], t)
            c, d = row_of(cols[h][i], t + 1), row_of(cols[h][i + 1], t + 1)
            r = reciprocal(a * d - b * c)
            ar, br, cr, dr = a * r, b * r, c * r, d * r

            def eliminate(col):
                x, y = row_of(col[h], t), row_of(col[h], t + 1)
                f, e = dr * x - br * y, ar * y - cr * x
                out = [col[k] - (cols[k][i] * f + cols[k][i + 1] * e) for k in range(parts)]
                out[h] = jnp.where(sub == t, f, jnp.where(sub == t + 1, e, out[h]))
                return out

            for j in range(i + 2, WIDTH):
                done = eliminate([cols[k][j] for k in range(parts)])
                for k in range(parts):
                    cols[k][j] = done[k]
            strip = eliminate(strip)
        near = [v for v in range(parts * (g + 1), parts * (g + 2)) if v < count]
        far = [v for v in range(count) if v not in near and v // parts != g]
        wide = [row_of(strip[i // SUB], i % SUB) for i in range(WIDTH)] if near else []
        for v in near:
            terms = [lane_of(rows[v], base + i) * wide[i] for i in range(WIDTH)]
            while len(terms) > 1:
                terms = [terms[k] + terms[k + 1] for k in range(0, len(terms), 2)]
            rows[v] = jnp.where(inside, 0.0, rows[v]) - terms[0]
        above = [jnp.zeros((base, BLOCK), f32)] if base else []
        below = [jnp.zeros((BLOCK - base - WIDTH, BLOCK), f32)] if base + WIDTH < BLOCK else []
        padded = jnp.concatenate(above + strip + below, 0)
        update = dot3(split(jnp.concatenate([rows[v] for v in far], 0)), split(padded))
        for k, v in enumerate(far):
            rows[v] = jnp.where(inside, 0.0, rows[v]) - update[k * SUB : (k + 1) * SUB]
        for h in range(parts):
            rows[parts * g + h] = strip[h]
    return jnp.concatenate(rows, 0)


def invert(ref):
    for j in range(PIV_BLOCKS):
        js = slice(j * BLOCK, (j + 1) * BLOCK)
        inverse = inverse_block(
            [ref[j * BLOCK + v * SUB : j * BLOCK + (v + 1) * SUB, js] for v in range(BLOCK // SUB)]
        )
        others = list(range(j + 1, PIV_BLOCKS)) + list(range(j))
        inverse_s = split(inverse)
        left = {i: split(ref[i * BLOCK : (i + 1) * BLOCK, js]) for i in others}
        top = {k: dot3(inverse_s, split(ref[js, k * BLOCK : (k + 1) * BLOCK])) for k in others}
        top_s = {k: split(top[k]) for k in others}
        for i in others:
            rows = slice(i * BLOCK, (i + 1) * BLOCK)
            for k in others:
                columns = slice(k * BLOCK, (k + 1) * BLOCK)
                ref[rows, columns] = ref[rows, columns] - dot3(left[i], top_s[k])
            ref[rows, js] = -dot3(left[i], inverse_s)
        for k in others:
            ref[js, k * BLOCK : (k + 1) * BLOCK] = top[k]
        ref[js, js] = inverse


def rows_at(index, count):
    return pl.ds(pl.multiple_of(index * count, SUB), count)


def place_panel(level, place, pieces, whole):
    count = PIECE_ROWS >> level
    x, core, leaf = place[0], place[1], place[2]
    for k in range(4):
        for c in range(2):
            for t in range(1 << level):
                owner = (leaf ^ t) * 8 + (x ^ k) * 2 + (core ^ c)
                whole[rows_at(owner, count), :] = pieces[k * 2 + c][t * count : (t + 1) * count, :]


def place_kernel(level, place, *refs):
    pieces, (pivot, below), (whole,) = refs[:8], refs[8:10], refs[10:]
    place_panel(level, place, pieces, whole)
    pivot[...] = whole[:PIV, :]
    below[...] = whole[PIV:, :]


def first_factor_kernel(place, *refs):
    pieces, (inverse, below), (whole,) = refs[:8], refs[8:10], refs[10:]
    place_panel(0, place, pieces, whole)
    inverse[...] = whole[:PIV, :]
    below[...] = whole[PIV:, :]
    invert(inverse)


def factor_kernel(place, pivot, mine, same, other, inverse, theirs):
    core = place[1]
    theirs[rows_at(core, HALF_ROWS), :] = same[...]
    theirs[rows_at(1 - core, HALF_ROWS), :] = other[...]
    for n, (p, q) in enumerate(LOWER):
        ps, qs = slice(p * BLOCK, (p + 1) * BLOCK), slice(q * BLOCK, (q + 1) * BLOCK)
        ns = slice(n * BLOCK, (n + 1) * BLOCK)
        total = pivot[ps, qs] + (mine[ns, :] + theirs[ns, :])
        inverse[ps, qs] = total
        if p != q:
            inverse[qs, ps] = total.T
    invert(inverse)


def block_of(ref, index_a, index_b):
    present = (index_a >= 0) & (index_b >= 0)
    spot = jnp.maximum(index_a, 0) * UPD_BLOCKS + jnp.maximum(index_b, 0)
    return jnp.where(present, ref[rows_at(spot, BLOCK), :], 0.0)


def extended(tables, level, mine, theirs, p, q):
    base = (level - 1) * 24
    own = block_of(mine, tables[base + p], tables[base + q])
    return own + block_of(theirs, tables[base + 12 + p], tables[base + 12 + q])


def mirror_shares(place, shares, packed, theirs):
    x, core = place[0], place[1]
    for k in range(4):
        for c in range(2):
            owner = (x ^ k) * 2 + (core ^ c)
            packed[rows_at(owner, SHARE_ROWS), :] = shares[k * 2 + c][...]
    for n, (a, b) in enumerate(PACKED):
        block = packed[n * BLOCK : (n + 1) * BLOCK, :]
        spot = (a * UPD_BLOCKS + b) * BLOCK
        theirs[spot : spot + BLOCK, :] = block
        if a != b:
            spot = (b * UPD_BLOCKS + a) * BLOCK
            theirs[spot : spot + BLOCK, :] = block.T


def assemble_below(level, tables, below, mine, theirs, columns):
    for u in range(UPD_BLOCKS):
        us = slice(u * BLOCK, (u + 1) * BLOCK)
        for q in range(PIV_BLOCKS):
            qs = slice(q * BLOCK, (q + 1) * BLOCK)
            columns[us, qs] = below[us, qs] + extended(tables, level, mine, theirs, PIV_BLOCKS + u, q)


def next_pivot(level, place, tables, mine, theirs, columns, weighted, parent, half):
    base = level * 24
    for n, (p, q) in enumerate(LOWER):
        a, b = tables[base + p], tables[base + q]
        a0, b0 = jnp.maximum(a, 0), jnp.maximum(b, 0)
        block = -dot3(
            split(weighted[rows_at(a0, BLOCK), :]), split(columns[rows_at(b0, BLOCK), :]), transposed=True
        )
        if level:
            block = block + extended(tables, level, mine, theirs, PIV_BLOCKS + a0, PIV_BLOCKS + b0)
        parent[n * BLOCK : (n + 1) * BLOCK, :] = jnp.where((a >= 0) & (b >= 0), block, 0.0)
    half[...] = parent[rows_at(place[1], HALF_ROWS), :]


def weigh(columns, inverse, weighted):
    inverse_s = split(inverse[...])
    for u in range(0, UPD, 256):
        weighted[u : u + 256, :] = dot3(split(columns[u : u + 256, :]), inverse_s)


def first_columns_kernel(place, tables, inverse, below, weighted, parent, half):
    weigh(below, inverse, weighted)
    next_pivot(0, place, tables, None, None, below, weighted, parent, half)


def columns_kernel(level, place, tables, inverse, below, mine, *refs):
    shares, (columns, weighted, parent, half, theirs), (packed,) = refs[:8], refs[8:13], refs[13:]
    mirror_shares(place, shares, packed, theirs)
    assemble_below(level, tables, below, mine, theirs, columns)
    weigh(columns, inverse, weighted)
    next_pivot(level, place, tables, mine, theirs, columns, weighted, parent, half)


def update_body(level, place, tables, columns, weighted, mine, theirs, update, share, packed):
    right = split(columns[...])
    for a in range(UPD_BLOCKS):
        left = split(weighted[a * BLOCK : (a + 1) * BLOCK, :])
        strip = dot3(left, right, transposed=True)
        for b in range(UPD_BLOCKS):
            block = -strip[:, b * BLOCK : (b + 1) * BLOCK]
            if level:
                block = block + extended(tables, level, mine, theirs, PIV_BLOCKS + a, PIV_BLOCKS + b)
            spot = (a * UPD_BLOCKS + b) * BLOCK
            update[spot : spot + BLOCK, :] = block
            if b <= a:
                n = PACKED.index((a, b))
                packed[n * BLOCK : (n + 1) * BLOCK, :] = block
    share[...] = packed[rows_at(place[0] * 2 + place[1], SHARE_ROWS), :]


def first_update_kernel(place, tables, columns, weighted, update, share, packed):
    update_body(0, place, tables, columns, weighted, None, None, update, share, packed)


def update_kernel(level, place, tables, columns, weighted, mine, theirs, update, share, packed):
    update_body(level, place, tables, columns, weighted, mine, theirs, update, share, packed)


def last_kernel(level, place, tables, inverse, below, mine, *refs):
    shares, (out,), (packed, theirs, columns) = refs[:8], refs[8:9], refs[9:]
    mirror_shares(place, shares, packed, theirs)
    assemble_below(level, tables, below, mine, theirs, columns)
    count = out.shape[0]
    position = place[2] * 8 + place[0] * 2 + place[1]
    per_block = BLOCK // count
    block_row, inner = position // per_block, position % per_block
    left = split(columns[rows_at(position, count), :])
    weighted = split(dot3(left, split(inverse[...])))
    strip = dot3(weighted, split(columns[...]), transposed=True)
    base = (level - 1) * 24

    def part(ref, index_a, index_b):
        present = (index_a >= 0) & (index_b >= 0)
        spot = (jnp.maximum(index_a, 0) * UPD_BLOCKS + jnp.maximum(index_b, 0)) * per_block + inner
        return jnp.where(present, ref[rows_at(spot, count), :], 0.0)

    for v in range(UPD_BLOCKS):
        mine_a, mine_b = tables[base + PIV_BLOCKS + block_row], tables[base + PIV_BLOCKS + v]
        their_a, their_b = tables[base + 12 + PIV_BLOCKS + block_row], tables[base + 12 + PIV_BLOCKS + v]
        vs = slice(v * BLOCK, (v + 1) * BLOCK)
        out[:, vs] = part(mine, mine_a, mine_b) + part(theirs, their_a, their_b) - strip[:, vs]


SMEM = pl.BlockSpec(memory_space=pltpu.SMEM)
VMEM = pl.BlockSpec(memory_space=pltpu.VMEM)


def call(kernel, name, scalars, arrays, outs, scratch, micros):
    shapes = [jax.ShapeDtypeStruct(shape, f32) for shape in outs]
    return pl.pallas_call(
        kernel,
        out_shape=shapes,
        in_specs=[SMEM] * len(scalars) + [VMEM] * len(arrays),
        out_specs=[VMEM] * len(outs),
        scratch_shapes=[pltpu.VMEM(shape, f32) for shape in scratch],
        compiler_params=pltpu.CompilerParams(vmem_limit_bytes=VMEM_BYTES),
        cost_estimate=pl.CostEstimate(flops=int(micros * 1.1e9), bytes_accessed=4096, transcendentals=0),
        name=name,
    )(*scalars, *arrays)


def flip(value, axis, mask):
    count = lax.axis_size(axis)
    return lax.ppermute(value, axis, [(i, i ^ mask) for i in range(count)])


def gather_row(value):
    chips = [value] + [flip(value, "row", 2 * k) for k in (1, 2, 3)]
    pieces = []
    for one in chips:
        pieces += [one, flip(one, "row", 1)]
    return pieces


def gather_panel(value, level):
    for bit in range(level):
        value = jnp.concatenate([value, flip(value, "leaf", 1 << bit)], axis=0)
    return gather_row(value)


def after(value, *others):
    return lax.optimization_barrier((value, *others))[0]


def inverse_map(blocks):
    spots = jnp.arange(FRONT // BLOCK, dtype=jnp.int32)
    order = jnp.arange(1, UPD_BLOCKS + 1, dtype=jnp.int32)
    return jnp.sum(jnp.where(blocks[:, None] == spots[None, :], order[:, None], 0), axis=0) - 1


def body(panel0, panel1, panel2, panel3, maps1, maps2, maps3):
    panels = (panel0, panel1, panel2, panel3)
    leaf = lax.axis_index("leaf")
    row = lax.axis_index("row")
    rows = []
    for level, maps in ((1, maps1), (2, maps2), (3, maps3)):
        child = leaf >> (level - 1)
        for front in (child, child ^ 1):
            rows.append(inverse_map(lax.dynamic_index_in_dim(maps, front, 0, keepdims=False)))
    tables = jnp.concatenate(rows)
    places = [jnp.stack([row // 2, row % 2, leaf % (1 << level)]).astype(jnp.int32) for level in range(4)]

    gathered = {0: gather_panel(panels[0], 0)}
    gathered[1] = gather_panel(after(panels[1], *gathered[0][1::2]), 1)
    gathered[2] = gather_panel(after(panels[2], *gathered[1][1::2]), 2)
    gathered[3] = gather_panel(after(panels[3], *gathered[2][1::2]), 3)

    inverse, below = call(
        first_factor_kernel, "factor0", [places[0]], gathered[0],
        [(PIV, PIV), (UPD, PIV)], [(FRONT, PIV)], 18,
    )
    weighted, parent, half = call(
        first_columns_kernel, "columns0", [places[0], tables], [inverse, below],
        [(UPD, PIV), (2 * HALF_ROWS, BLOCK), (HALF_ROWS, BLOCK)], [], 6,
    )
    update, share = call(
        first_update_kernel, "update0", [places[0], tables], [below, weighted],
        [(UPD_BLOCKS * UPD, BLOCK), (SHARE_ROWS, BLOCK)], [(len(PACKED) * BLOCK, BLOCK)], 6,
    )
    for level in (1, 2, 3):
        bit = 1 << (level - 1)
        same = flip(half, "leaf", bit)
        other = flip(same, "row", 1)
        shares = gather_row(flip(share, "leaf", bit))
        pivot, below = call(
            functools.partial(place_kernel, level), f"place{level}", [places[level]], gathered[level],
            [(PIV, PIV), (UPD, PIV)], [(FRONT, PIV)], 3,
        )
        inverse = call(
            factor_kernel, f"factor{level}", [places[level]], [pivot, parent, same, other],
            [(PIV, PIV)], [(2 * HALF_ROWS, BLOCK)], 18,
        )[0]
        if level == 3:
            return call(
                functools.partial(last_kernel, level), "last", [places[level], tables],
                [inverse, below, update, *shares], [(UPD // 64, UPD)],
                [(len(PACKED) * BLOCK, BLOCK), (UPD_BLOCKS * UPD, BLOCK), (UPD, PIV)], 8,
            )[0]
        columns, weighted, parent, half, theirs = call(
            functools.partial(columns_kernel, level), f"columns{level}", [places[level], tables],
            [inverse, below, update, *shares],
            [(UPD, PIV), (UPD, PIV), (2 * HALF_ROWS, BLOCK), (HALF_ROWS, BLOCK), (UPD_BLOCKS * UPD, BLOCK)],
            [(len(PACKED) * BLOCK, BLOCK)], 10,
        )
        update, share = call(
            functools.partial(update_kernel, level), f"update{level}", [places[level], tables],
            [columns, weighted, update, theirs],
            [(UPD_BLOCKS * UPD, BLOCK), (SHARE_ROWS, BLOCK)], [(len(PACKED) * BLOCK, BLOCK)], 8,
        )


def solution(mesh):
    panel = P(("leaf", "row"), None)
    return jax.shard_map(
        body, mesh=mesh, in_specs=(panel,) * 4 + (P(),) * 3, out_specs=panel, check_vma=False
    )
```

```python
import functools

import jax
import jax.numpy as jnp
from jax import lax
from jax.experimental import pallas as pl
from jax.experimental.pallas import tpu as pltpu
from jax.sharding import PartitionSpec as P

BLOCK = 128
PIV = 512
UPD = 1024
FRONT = PIV + UPD
SUB = 8
WIDTH = 16
PIV_BLOCKS = PIV // BLOCK
UPD_BLOCKS = UPD // BLOCK
PIECE_ROWS = 192
LOWER = [(p, q) for p in range(PIV_BLOCKS) for q in range(p + 1)]
PACKED = [(a, b) for a in range(UPD_BLOCKS) for b in range(a + 1)]
HALF_ROWS = len(LOWER) * BLOCK // 2
SHARE_ROWS = len(PACKED) * BLOCK // 2
MIB = 1024 * 1024

f32 = jnp.float32
bf16 = jnp.bfloat16


def split(x):
    high = x.astype(bf16)
    return high, (x - high.astype(f32)).astype(bf16)


def dot3(left, right, transposed=False):
    dims = (((1,), (1 if transposed else 0,)), ((), ()))
    dot = functools.partial(lax.dot_general, dimension_numbers=dims, preferred_element_type=f32)
    return dot(left[0], right[0]) + (dot(left[0], right[1]) + dot(left[1], right[0]))


def reciprocal(x):
    r = pltpu.reciprocal(x, approx=True)
    return r * (2.0 - x * r)


def inverse_block(rows):
    count = len(rows)
    parts = WIDTH // SUB
    shape = (SUB, BLOCK)
    lane = lax.broadcasted_iota(jnp.int32, shape, 1)
    sub = lax.broadcasted_iota(jnp.int32, shape, 0)
    rows = list(rows)

    def row_of(x, t):
        return jnp.broadcast_to(x[t : t + 1, :], shape)

    def lane_of(x, l):
        return jnp.broadcast_to(x[:, l : l + 1], shape)

    for g in range(count // parts):
        base = g * WIDTH
        inside = (lane >= base) & (lane < base + WIDTH)
        cols = [[lane_of(rows[parts * g + h], base + i) for i in range(WIDTH)] for h in range(parts)]
        strip = [
            jnp.where(inside, jnp.where(lane == base + h * SUB + sub, 1.0, 0.0), rows[parts * g + h])
            for h in range(parts)
        ]
        for i in range(0, WIDTH, 2):
            h, t = i // SUB, i % SUB
            a, b = row_of(cols[h][i], t), row_of(cols[h][i + 1], t)
            c, d = row_of(cols[h][i], t + 1), row_of(cols[h][i + 1], t + 1)
            r = reciprocal(a * d - b * c)
            ar, br, cr, dr = a * r, b * r, c * r, d * r

            def eliminate(col):
                x, y = row_of(col[h], t), row_of(col[h], t + 1)
                f, e = dr * x - br * y, ar * y - cr * x
                out = [col[k] - (cols[k][i] * f + cols[k][i + 1] * e) for k in range(parts)]
                out[h] = jnp.where(sub == t, f, jnp.where(sub == t + 1, e, out[h]))
                return out

            for j in range(i + 2, WIDTH):
                done = eliminate([cols[k][j] for k in range(parts)])
                for k in range(parts):
                    cols[k][j] = done[k]
            strip = eliminate(strip)
        near = [v for v in range(parts * (g + 1), parts * (g + 2)) if v < count]
        far = [v for v in range(count) if v not in near and v // parts != g]
        wide = [row_of(strip[i // SUB], i % SUB) for i in range(WIDTH)] if near else []
        for v in near:
            terms = [lane_of(rows[v], base + i) * wide[i] for i in range(WIDTH)]
            while len(terms) > 1:
                terms = [terms[k] + terms[k + 1] for k in range(0, len(terms), 2)]
            rows[v] = jnp.where(inside, 0.0, rows[v]) - terms[0]
        above = [jnp.zeros((base, BLOCK), f32)] if base else []
        below = [jnp.zeros((BLOCK - base - WIDTH, BLOCK), f32)] if base + WIDTH < BLOCK else []
        padded = jnp.concatenate(above + strip + below, 0)
        update = dot3(split(jnp.concatenate([rows[v] for v in far], 0)), split(padded))
        for k, v in enumerate(far):
            rows[v] = jnp.where(inside, 0.0, rows[v]) - update[k * SUB : (k + 1) * SUB]
        for h in range(parts):
            rows[parts * g + h] = strip[h]
    return jnp.concatenate(rows, 0)


def invert(ref):
    for j in range(PIV_BLOCKS):
        js = slice(j * BLOCK, (j + 1) * BLOCK)
        inverse = inverse_block(
            [ref[j * BLOCK + v * SUB : j * BLOCK + (v + 1) * SUB, js] for v in range(BLOCK // SUB)]
        )
        others = list(range(j + 1, PIV_BLOCKS)) + list(range(j))
        inverse_s = split(inverse)
        left = {i: split(ref[i * BLOCK : (i + 1) * BLOCK, js]) for i in others}
        top = {k: dot3(inverse_s, split(ref[js, k * BLOCK : (k + 1) * BLOCK])) for k in others}
        top_s = {k: split(top[k]) for k in others}
        for i in others:
            rows = slice(i * BLOCK, (i + 1) * BLOCK)
            for k in others:
                columns = slice(k * BLOCK, (k + 1) * BLOCK)
                ref[rows, columns] = ref[rows, columns] - dot3(left[i], top_s[k])
            ref[rows, js] = -dot3(left[i], inverse_s)
        for k in others:
            ref[js, k * BLOCK : (k + 1) * BLOCK] = top[k]
        ref[js, js] = inverse


def rows_at(index, count):
    return pl.ds(pl.multiple_of(index * count, SUB), count)


def place_panel(level, place, gathered, whole):
    count = PIECE_ROWS >> level
    for row in range(8):
        for t in range(1 << level):
            owner = (place[2] ^ t) * 8 + row
            start = row * PIECE_ROWS + t * count
            whole[rows_at(owner, count), :] = gathered[start : start + count, :]


def first_factor_kernel(place, *refs):
    pieces, (inverse, below), (whole,) = refs[:10], refs[10:12], refs[12:]
    half = PIECE_ROWS // 2
    for k, first, count, spot in ((0, 0, 2, 0), (1, 0, 2, 1), (3, 0, 2, 2), (2, 0, 1, 3), (2, 1, 1, 4)):
        for c in range(2):
            owner = ((place[0] ^ k) * 2 + (place[1] ^ c)) * 2 + first
            rows = pl.ds(pl.multiple_of(owner * half, SUB), count * half)
            whole[rows, :] = pieces[spot * 2 + c][...]
    inverse[...] = whole[:PIV, :]
    below[...] = whole[PIV:, :]
    invert(inverse)


def factor_kernel(level, place, gathered, mine, same, other, inverse, below, theirs, whole):
    core = place[1]
    place_panel(level, place, gathered, whole)
    below[...] = whole[PIV:, :]
    theirs[rows_at(core, HALF_ROWS), :] = same[...]
    theirs[rows_at(1 - core, HALF_ROWS), :] = other[...]
    for n, (p, q) in enumerate(LOWER):
        ps, qs = slice(p * BLOCK, (p + 1) * BLOCK), slice(q * BLOCK, (q + 1) * BLOCK)
        ns = slice(n * BLOCK, (n + 1) * BLOCK)
        total = whole[ps, qs] + (mine[ns, :] + theirs[ns, :])
        inverse[ps, qs] = total
        if p != q:
            inverse[qs, ps] = total.T
    invert(inverse)


def block_of(ref, index_a, index_b):
    present = (index_a >= 0) & (index_b >= 0)
    spot = jnp.maximum(index_a, 0) * UPD_BLOCKS + jnp.maximum(index_b, 0)
    return jnp.where(present, ref[rows_at(spot, BLOCK), :], 0.0)


def extended(tables, level, mine, theirs, p, q):
    base = (level - 1) * 24
    own = block_of(mine, tables[base + p], tables[base + q])
    return own + block_of(theirs, tables[base + 12 + p], tables[base + 12 + q])


def mirror_shares(place, same, other, packed, theirs):
    core = place[1]
    packed[rows_at(core, SHARE_ROWS), :] = same[...]
    packed[rows_at(1 - core, SHARE_ROWS), :] = other[...]
    for n, (a, b) in enumerate(PACKED):
        block = packed[n * BLOCK : (n + 1) * BLOCK, :]
        spot = (a * UPD_BLOCKS + b) * BLOCK
        theirs[spot : spot + BLOCK, :] = block
        if a != b:
            spot = (b * UPD_BLOCKS + a) * BLOCK
            theirs[spot : spot + BLOCK, :] = block.T


def assemble_below(level, tables, below, mine, theirs, columns):
    for u in range(UPD_BLOCKS):
        us = slice(u * BLOCK, (u + 1) * BLOCK)
        for q in range(PIV_BLOCKS):
            qs = slice(q * BLOCK, (q + 1) * BLOCK)
            columns[us, qs] = below[us, qs] + extended(tables, level, mine, theirs, PIV_BLOCKS + u, q)


def next_pivot(level, place, tables, trailing, columns, weighted, parent, half):
    base = level * 24
    for n, (p, q) in enumerate(LOWER):
        a, b = tables[base + p], tables[base + q]
        a0, b0 = jnp.maximum(a, 0), jnp.maximum(b, 0)
        block = -dot3(
            split(weighted[rows_at(a0, BLOCK), :]), split(columns[rows_at(b0, BLOCK), :]), transposed=True
        )
        if level:
            block = block + trailing[rows_at(a0 * UPD_BLOCKS + b0, BLOCK), :]
        parent[n * BLOCK : (n + 1) * BLOCK, :] = jnp.where((a >= 0) & (b >= 0), block, 0.0)
    half[...] = parent[rows_at(place[1], HALF_ROWS), :]


def weigh(columns, inverse, weighted):
    inverse_s = split(inverse[...])
    for u in range(0, UPD, 256):
        weighted[u : u + 256, :] = dot3(split(columns[u : u + 256, :]), inverse_s)


def first_columns_kernel(place, tables, inverse, below, weighted, parent, half):
    weigh(below, inverse, weighted)
    next_pivot(0, place, tables, None, below, weighted, parent, half)


def columns_kernel(
    level, place, tables, inverse, below, mine, same, other,
    columns, weighted, parent, half, trailing, packed, theirs,
):
    mirror_shares(place, same, other, packed, theirs)
    assemble_below(level, tables, below, mine, theirs, columns)
    weigh(columns, inverse, weighted)
    for a in range(UPD_BLOCKS):
        for b in range(UPD_BLOCKS):
            spot = (a * UPD_BLOCKS + b) * BLOCK
            trailing[spot : spot + BLOCK, :] = extended(
                tables, level, mine, theirs, PIV_BLOCKS + a, PIV_BLOCKS + b
            )
    next_pivot(level, place, tables, trailing, columns, weighted, parent, half)


def update_body(place, columns, weighted, trailing, update, share, packed):
    left = split(weighted[...])
    step = 2 * BLOCK
    for start in range(0, UPD, step):
        strip = dot3(left, split(columns[start : start + step, :]), transposed=True)
        for a in range(UPD_BLOCKS):
            for inner in range(2):
                b = start // BLOCK + inner
                spot = (a * UPD_BLOCKS + b) * BLOCK
                block = -strip[a * BLOCK : (a + 1) * BLOCK, inner * BLOCK : (inner + 1) * BLOCK]
                if trailing is not None:
                    block = trailing[spot : spot + BLOCK, :] + block
                update[spot : spot + BLOCK, :] = block
                if b <= a:
                    n = PACKED.index((a, b))
                    packed[n * BLOCK : (n + 1) * BLOCK, :] = block
    share[...] = packed[rows_at(place[1], SHARE_ROWS), :]


def first_update_kernel(place, columns, weighted, update, share, packed):
    update_body(place, columns, weighted, None, update, share, packed)


def update_kernel(place, columns, weighted, trailing, update, share, packed):
    update_body(place, columns, weighted, trailing, update, share, packed)


def last_kernel(level, place, tables, inverse, below, mine, same, other, out, packed, theirs, columns):
    mirror_shares(place, same, other, packed, theirs)
    assemble_below(level, tables, below, mine, theirs, columns)
    count = out.shape[0]
    position = place[2] * 8 + place[0] * 2 + place[1]
    per_block = BLOCK // count
    block_row, inner = position // per_block, position % per_block
    left = split(columns[rows_at(position, count), :])
    weighted = split(dot3(left, split(inverse[...])))
    strip = dot3(weighted, split(columns[...]), transposed=True)
    base = (level - 1) * 24

    def part(ref, index_a, index_b):
        present = (index_a >= 0) & (index_b >= 0)
        spot = (jnp.maximum(index_a, 0) * UPD_BLOCKS + jnp.maximum(index_b, 0)) * per_block + inner
        return jnp.where(present, ref[rows_at(spot, count), :], 0.0)

    for v in range(UPD_BLOCKS):
        mine_a, mine_b = tables[base + PIV_BLOCKS + block_row], tables[base + PIV_BLOCKS + v]
        their_a, their_b = tables[base + 12 + PIV_BLOCKS + block_row], tables[base + 12 + PIV_BLOCKS + v]
        vs = slice(v * BLOCK, (v + 1) * BLOCK)
        out[:, vs] = part(mine, mine_a, mine_b) + part(theirs, their_a, their_b) - strip[:, vs]


SMEM = pl.BlockSpec(memory_space=pltpu.SMEM)
VMEM = pl.BlockSpec(memory_space=pltpu.VMEM)


def call(kernel, name, scalars, arrays, outs, scratch, micros, mib):
    shapes = [jax.ShapeDtypeStruct(shape, f32) for shape in outs]
    return pl.pallas_call(
        kernel,
        out_shape=shapes,
        in_specs=[SMEM] * len(scalars) + [VMEM] * len(arrays),
        out_specs=[VMEM] * len(outs),
        scratch_shapes=[pltpu.VMEM(shape, f32) for shape in scratch],
        compiler_params=pltpu.CompilerParams(vmem_limit_bytes=mib * MIB),
        cost_estimate=pl.CostEstimate(flops=int(micros * 1.1e9), bytes_accessed=4096, transcendentals=0),
        name=name,
    )(*scalars, *arrays)


def flip(value, axis, mask):
    count = lax.axis_size(axis)
    return lax.ppermute(value, axis, [(i, i ^ mask) for i in range(count)])


def gather_first(value):
    middle = PIECE_ROWS // 2
    near, far = flip(value, "row", 2), flip(value, "row", 6)
    parts = [value, near, far, flip(near[:middle], "row", 6), flip(far[middle:], "row", 2)]
    pieces = []
    for part in parts:
        pieces += [part, flip(part, "row", 1)]
    return pieces


def wider(value, bit):
    return jnp.concatenate([value, flip(value, "leaf", 1 << bit)], axis=0)


def gather_row(value):
    return lax.all_gather(value, "row", axis=0, tiled=True)


def inverse_map(blocks):
    spots = jnp.arange(FRONT // BLOCK, dtype=jnp.int32)
    order = jnp.arange(1, UPD_BLOCKS + 1, dtype=jnp.int32)
    return jnp.sum(jnp.where(blocks[:, None] == spots[None, :], order[:, None], 0), axis=0) - 1


def body(panel0, panel1, panel2, panel3, maps1, maps2, maps3):
    panels = (panel0, panel1, panel2, panel3)
    leaf = lax.axis_index("leaf")
    row = lax.axis_index("row")
    rows = []
    for level, maps in ((1, maps1), (2, maps2), (3, maps3)):
        child = leaf >> (level - 1)
        for front in (child, child ^ 1):
            rows.append(inverse_map(lax.dynamic_index_in_dim(maps, front, 0, keepdims=False)))
    tables = jnp.concatenate(rows)
    places = [jnp.stack([row // 2, row % 2, leaf % (1 << level)]).astype(jnp.int32) for level in range(4)]

    pieces = gather_first(panels[0])
    leaf1, leaf2, leaf3 = [wider(panels[level], 0) for level in (1, 2, 3)]
    *pieces, leaf1, leaf2, leaf3 = lax.optimization_barrier((*pieces, leaf1, leaf2, leaf3))
    gathered = {1: gather_row(leaf1)}
    flipped2, flipped3 = flip(leaf2, "leaf", 2), flip(leaf3, "leaf", 2)

    inverse, below = call(
        first_factor_kernel, "factor0", [places[0]], pieces,
        [(PIV, PIV), (UPD, PIV)], [(FRONT, PIV)], 18, 16,
    )
    weighted, parent, half = call(
        first_columns_kernel, "columns0", [places[0], tables], [inverse, below],
        [(UPD, PIV), (2 * HALF_ROWS, BLOCK), (HALF_ROWS, BLOCK)], [], 5, 16,
    )
    update, share = call(
        first_update_kernel, "update0", [places[0]], [below, weighted],
        [(UPD_BLOCKS * UPD, BLOCK), (SHARE_ROWS, BLOCK)], [(len(PACKED) * BLOCK, BLOCK)], 5, 20,
    )
    for level in (1, 2, 3):
        bit = 1 << (level - 1)
        same = flip(half, "leaf", bit)
        same, share = lax.optimization_barrier((same, share))
        other = flip(same, "row", 1)
        same_share = flip(share, "leaf", bit)
        if level == 1:
            flipped2, flipped3, share = lax.optimization_barrier((flipped2, flipped3, share))
            gathered[2] = gather_row(jnp.concatenate([leaf2, flipped2], axis=0))
            leaf3 = jnp.concatenate([leaf3, flipped3], axis=0)
            flipped3 = flip(leaf3, "leaf", 4)
        if level == 2:
            flipped3, share = lax.optimization_barrier((flipped3, share))
            gathered[3] = gather_row(jnp.concatenate([leaf3, flipped3], axis=0))
        inverse, below = call(
            functools.partial(factor_kernel, level), f"factor{level}", [places[level]],
            [gathered[level], parent, same, other],
            [(PIV, PIV), (UPD, PIV)], [(2 * HALF_ROWS, BLOCK), (FRONT, PIV)], 18, 16,
        )
        same_share, inverse = lax.optimization_barrier((same_share, inverse))
        other_share = flip(same_share, "row", 1)
        if level == 3:
            return call(
                functools.partial(last_kernel, level), "last", [places[level], tables],
                [inverse, below, update, same_share, other_share], [(UPD // 64, UPD)],
                [(len(PACKED) * BLOCK, BLOCK), (UPD_BLOCKS * UPD, BLOCK), (UPD, PIV)], 5, 26,
            )[0]
        columns, weighted, parent, half, trailing = call(
            functools.partial(columns_kernel, level), f"columns{level}", [places[level], tables],
            [inverse, below, update, same_share, other_share],
            [(UPD, PIV), (UPD, PIV), (2 * HALF_ROWS, BLOCK), (HALF_ROWS, BLOCK), (UPD_BLOCKS * UPD, BLOCK)],
            [(len(PACKED) * BLOCK, BLOCK), (UPD_BLOCKS * UPD, BLOCK)], 8, 32,
        )
        update, share = call(
            update_kernel, f"update{level}", [places[level]],
            [columns, weighted, trailing],
            [(UPD_BLOCKS * UPD, BLOCK), (SHARE_ROWS, BLOCK)], [(len(PACKED) * BLOCK, BLOCK)], 5, 24,
        )


def solution(mesh):
    panel = P(("leaf", "row"), None)
    return jax.shard_map(
        body, mesh=mesh, in_specs=(panel,) * 4 + (P(),) * 3, out_specs=panel, check_vma=False
    )
```

```python
import functools

import jax
import jax.numpy as jnp
from jax import lax
from jax.experimental import pallas as pl
from jax.experimental.pallas import tpu as pltpu
from jax.sharding import PartitionSpec as P

BLOCK = 128
PIV = 512
UPD = 1024
FRONT = PIV + UPD
SUB = 8
WIDTH = 16
PIV_BLOCKS = PIV // BLOCK
UPD_BLOCKS = UPD // BLOCK
PIECE_ROWS = 192
LOWER = [(p, q) for p in range(PIV_BLOCKS) for q in range(p + 1)]
REST = [(a, b) for a in range(PIV_BLOCKS, UPD_BLOCKS) for b in range(a + 1)]
HALF_ROWS = len(LOWER) * BLOCK // 2
SHARE_ROWS = len(REST) * BLOCK // 2
TABLE = 32
RANK = 12
ORDER = 24
MIB = 1024 * 1024

f32 = jnp.float32
bf16 = jnp.bfloat16


def split(x):
    high = x.astype(bf16)
    return high, (x - high.astype(f32)).astype(bf16)


def dot3(left, right, transposed=False):
    dims = (((1,), (1 if transposed else 0,)), ((), ()))
    dot = functools.partial(lax.dot_general, dimension_numbers=dims, preferred_element_type=f32)
    return dot(left[0], right[0]) + (dot(left[0], right[1]) + dot(left[1], right[0]))


def reciprocal(x):
    return 1.0 / x


def inverse_block(rows):
    count = len(rows)
    parts = WIDTH // SUB
    shape = (SUB, BLOCK)
    lane = lax.broadcasted_iota(jnp.int32, shape, 1)
    sub = lax.broadcasted_iota(jnp.int32, shape, 0)
    rows = list(rows)

    def row_of(x, t):
        return jnp.broadcast_to(x[t : t + 1, :], shape)

    def lane_of(x, l):
        return jnp.broadcast_to(x[:, l : l + 1], shape)

    for g in range(count // parts):
        base = g * WIDTH
        inside = (lane >= base) & (lane < base + WIDTH)
        cols = [[lane_of(rows[parts * g + h], base + i) for i in range(WIDTH)] for h in range(parts)]
        strip = [
            jnp.where(inside, jnp.where(lane == base + h * SUB + sub, 1.0, 0.0), rows[parts * g + h])
            for h in range(parts)
        ]
        for i in range(0, WIDTH, 2):
            h, t = i // SUB, i % SUB
            a, b = row_of(cols[h][i], t), row_of(cols[h][i + 1], t)
            c, d = row_of(cols[h][i], t + 1), row_of(cols[h][i + 1], t + 1)
            r = reciprocal(a * d - b * c)
            ar, br, cr, dr = a * r, b * r, c * r, d * r

            def eliminate(col):
                x, y = row_of(col[h], t), row_of(col[h], t + 1)
                f, e = dr * x - br * y, ar * y - cr * x
                out = [col[k] - (cols[k][i] * f + cols[k][i + 1] * e) for k in range(parts)]
                out[h] = jnp.where(sub == t, f, jnp.where(sub == t + 1, e, out[h]))
                return out

            for j in range(i + 2, WIDTH):
                done = eliminate([cols[k][j] for k in range(parts)])
                for k in range(parts):
                    cols[k][j] = done[k]
            strip = eliminate(strip)
        near = [v for v in range(parts * (g + 1), parts * (g + 2)) if v < count]
        far = [v for v in range(count) if v not in near and v // parts != g]
        wide = [row_of(strip[i // SUB], i % SUB) for i in range(WIDTH)] if near else []
        for v in near:
            terms = [lane_of(rows[v], base + i) * wide[i] for i in range(WIDTH)]
            while len(terms) > 1:
                terms = [terms[k] + terms[k + 1] for k in range(0, len(terms), 2)]
            rows[v] = jnp.where(inside, 0.0, rows[v]) - terms[0]
        above = [jnp.zeros((base, BLOCK), f32)] if base else []
        below = [jnp.zeros((BLOCK - base - WIDTH, BLOCK), f32)] if base + WIDTH < BLOCK else []
        padded = jnp.concatenate(above + strip + below, 0)
        update = dot3(split(jnp.concatenate([rows[v] for v in far], 0)), split(padded))
        for k, v in enumerate(far):
            rows[v] = jnp.where(inside, 0.0, rows[v]) - update[k * SUB : (k + 1) * SUB]
        for h in range(parts):
            rows[parts * g + h] = strip[h]
    return jnp.concatenate(rows, 0)


def invert(ref):
    for j in range(PIV_BLOCKS):
        js = slice(j * BLOCK, (j + 1) * BLOCK)
        inverse = inverse_block(
            [ref[j * BLOCK + v * SUB : j * BLOCK + (v + 1) * SUB, js] for v in range(BLOCK // SUB)]
        )
        others = list(range(j + 1, PIV_BLOCKS)) + list(range(j))
        inverse_s = split(inverse)
        left = {i: split(ref[i * BLOCK : (i + 1) * BLOCK, js]) for i in others}
        top = {k: dot3(inverse_s, split(ref[js, k * BLOCK : (k + 1) * BLOCK])) for k in others}
        top_s = {k: split(top[k]) for k in others}
        for i in others:
            rows = slice(i * BLOCK, (i + 1) * BLOCK)
            for k in others:
                columns = slice(k * BLOCK, (k + 1) * BLOCK)
                ref[rows, columns] = ref[rows, columns] - dot3(left[i], top_s[k])
            ref[rows, js] = -dot3(left[i], inverse_s)
        for k in others:
            ref[js, k * BLOCK : (k + 1) * BLOCK] = top[k]
        ref[js, js] = inverse


def rows_at(index, count):
    return pl.ds(pl.multiple_of(index * count, SUB), count)


def place_kernel(level, place, gathered, pivot, below, whole):
    count = PIECE_ROWS >> level
    for row in range(8):
        for t in range(1 << level):
            owner = (place[2] ^ t) * 8 + row
            start = row * PIECE_ROWS + t * count
            whole[rows_at(owner, count), :] = gathered[start : start + count, :]
    pivot[...] = whole[:PIV, :]
    below[...] = whole[PIV:, :]


def first_place_kernel(place, *refs):
    pieces, (pivot, below), (whole,) = refs[:10], refs[10:12], refs[12:]
    half = PIECE_ROWS // 2
    for k, first, count, spot in ((0, 0, 2, 0), (1, 0, 2, 1), (3, 0, 2, 2), (2, 0, 1, 3), (2, 1, 1, 4)):
        for c in range(2):
            owner = ((place[0] ^ k) * 2 + (place[1] ^ c)) * 2 + first
            rows = pl.ds(pl.multiple_of(owner * half, SUB), count * half)
            whole[rows, :] = pieces[spot * 2 + c][...]
    pivot[...] = whole[:PIV, :]
    below[...] = whole[PIV:, :]


def first_factor_kernel(pivot, inverse):
    inverse[...] = pivot[...]
    invert(inverse)


def join(place, same, other, both):
    count = same.shape[0]
    both[rows_at(place[1], count), :] = same[...]
    both[rows_at(1 - place[1], count), :] = other[...]


def leading(ref, i, j):
    i0, j0 = jnp.maximum(i, 0), jnp.maximum(j, 0)
    spot = lax.shift_right_logical(i0 * (i0 + 1), 1) + j0
    return jnp.where((i >= 0) & (j >= 0), ref[rows_at(spot, BLOCK), :], 0.0)


def factor_kernel(level, place, tables, pivot, mine, same, other, inverse, theirs):
    join(place, same, other, theirs)
    own = (level - 1) * 2 * TABLE + RANK
    for p, q in LOWER:
        ps, qs = slice(p * BLOCK, (p + 1) * BLOCK), slice(q * BLOCK, (q + 1) * BLOCK)
        added = leading(mine, tables[own + p], tables[own + q])
        added = added + leading(theirs, tables[own + TABLE + p], tables[own + TABLE + q])
        total = pivot[ps, qs] + added
        inverse[ps, qs] = total
        if p != q:
            inverse[qs, ps] = total.T
    invert(inverse)


def block_of(ref, index_a, index_b):
    present = (index_a >= 0) & (index_b >= 0)
    spot = jnp.maximum(index_a, 0) * UPD_BLOCKS + jnp.maximum(index_b, 0)
    return jnp.where(present, ref[rows_at(spot, BLOCK), :], 0.0)


def extended(tables, level, mine, theirs, p, q):
    own = (level - 1) * 2 * TABLE
    other = own + TABLE + RANK
    return block_of(mine, tables[own + p], tables[own + q]) + block_of(
        theirs, tables[other + p], tables[other + q]
    )


def mirror(place, lead_same, lead_other, rest_same, rest_other, lead, rest, theirs):
    join(place, lead_same, lead_other, lead)
    join(place, rest_same, rest_other, rest)
    for pairs, ref in ((LOWER, lead), (REST, rest)):
        for n, (a, b) in enumerate(pairs):
            block = ref[n * BLOCK : (n + 1) * BLOCK, :]
            spot = (a * UPD_BLOCKS + b) * BLOCK
            theirs[spot : spot + BLOCK, :] = block
            if a != b:
                spot = (b * UPD_BLOCKS + a) * BLOCK
                theirs[spot : spot + BLOCK, :] = block.T


def assemble_below(level, tables, below, mine, theirs, columns):
    for u in range(UPD_BLOCKS):
        us = slice(u * BLOCK, (u + 1) * BLOCK)
        for q in range(PIV_BLOCKS):
            qs = slice(q * BLOCK, (q + 1) * BLOCK)
            columns[us, qs] = below[us, qs] + extended(tables, level, mine, theirs, PIV_BLOCKS + u, q)


def lead_blocks(level, place, tables, trailing, columns, weighted, lead, half):
    order = level * 2 * TABLE + ORDER
    for n, (i, j) in enumerate(LOWER):
        a, b = tables[order + i], tables[order + j]
        block = -dot3(
            split(weighted[rows_at(a, BLOCK), :]), split(columns[rows_at(b, BLOCK), :]), transposed=True
        )
        if level:
            block = block + trailing[rows_at(a * UPD_BLOCKS + b, BLOCK), :]
        lead[n * BLOCK : (n + 1) * BLOCK, :] = block
    half[...] = lead[rows_at(place[1], HALF_ROWS), :]


def weigh(columns, inverse, weighted):
    inverse_s = split(inverse[...])
    for u in range(0, UPD, 256):
        weighted[u : u + 256, :] = dot3(split(columns[u : u + 256, :]), inverse_s)


def first_columns_kernel(place, tables, inverse, below, weighted, parent, half):
    weigh(below, inverse, weighted)
    lead_blocks(0, place, tables, None, below, weighted, parent, half)


def columns_kernel(
    level, place, tables, inverse, below, mine, lead_same, lead_other, rest_same, rest_other,
    columns, weighted, parent, half, trailing, lead, rest, theirs,
):
    mirror(place, lead_same, lead_other, rest_same, rest_other, lead, rest, theirs)
    assemble_below(level, tables, below, mine, theirs, columns)
    weigh(columns, inverse, weighted)
    for a in range(UPD_BLOCKS):
        for b in range(UPD_BLOCKS):
            spot = (a * UPD_BLOCKS + b) * BLOCK
            trailing[spot : spot + BLOCK, :] = extended(
                tables, level, mine, theirs, PIV_BLOCKS + a, PIV_BLOCKS + b
            )
    lead_blocks(level, place, tables, trailing, columns, weighted, parent, half)


def update_body(level, place, tables, columns, weighted, trailing, update, share):
    left = split(weighted[...])
    step = 2 * BLOCK
    for start in range(0, UPD, step):
        strip = dot3(left, split(columns[start : start + step, :]), transposed=True)
        for a in range(UPD_BLOCKS):
            for inner in range(2):
                b = start // BLOCK + inner
                spot = (a * UPD_BLOCKS + b) * BLOCK
                block = -strip[a * BLOCK : (a + 1) * BLOCK, inner * BLOCK : (inner + 1) * BLOCK]
                if trailing is not None:
                    block = trailing[spot : spot + BLOCK, :] + block
                update[spot : spot + BLOCK, :] = block
    order = level * 2 * TABLE + ORDER
    count = len(REST) // 2
    for n in range(count):
        (i0, j0), (i1, j1) = REST[n], REST[count + n]
        a = tables[order + i0 + place[1] * (i1 - i0)]
        b = tables[order + j0 + place[1] * (j1 - j0)]
        share[n * BLOCK : (n + 1) * BLOCK, :] = update[rows_at(a * UPD_BLOCKS + b, BLOCK), :]


def first_update_kernel(place, tables, columns, weighted, update, share):
    update_body(0, place, tables, columns, weighted, None, update, share)


def last_kernel(
    level, place, tables, inverse, below, mine, lead_same, lead_other, rest_same, rest_other,
    out, lead, rest, theirs, columns,
):
    mirror(place, lead_same, lead_other, rest_same, rest_other, lead, rest, theirs)
    assemble_below(level, tables, below, mine, theirs, columns)
    count = out.shape[0]
    position = place[2] * 8 + place[0] * 2 + place[1]
    per_block = BLOCK // count
    block_row, inner = position // per_block, position % per_block
    left = split(columns[rows_at(position, count), :])
    weighted = split(dot3(left, split(inverse[...])))
    strip = dot3(weighted, split(columns[...]), transposed=True)
    own = (level - 1) * 2 * TABLE
    sibling = own + TABLE + RANK

    def part(ref, index_a, index_b):
        present = (index_a >= 0) & (index_b >= 0)
        spot = (jnp.maximum(index_a, 0) * UPD_BLOCKS + jnp.maximum(index_b, 0)) * per_block + inner
        return jnp.where(present, ref[rows_at(spot, count), :], 0.0)

    for v in range(UPD_BLOCKS):
        mine_a, mine_b = tables[own + PIV_BLOCKS + block_row], tables[own + PIV_BLOCKS + v]
        their_a, their_b = tables[sibling + PIV_BLOCKS + block_row], tables[sibling + PIV_BLOCKS + v]
        vs = slice(v * BLOCK, (v + 1) * BLOCK)
        out[:, vs] = part(mine, mine_a, mine_b) + part(theirs, their_a, their_b) - strip[:, vs]


SMEM = pl.BlockSpec(memory_space=pltpu.SMEM)
VMEM = pl.BlockSpec(memory_space=pltpu.VMEM)


def call(kernel, name, scalars, arrays, outs, scratch, micros, mib):
    shapes = [jax.ShapeDtypeStruct(shape, f32) for shape in outs]
    return pl.pallas_call(
        kernel,
        out_shape=shapes,
        in_specs=[SMEM] * len(scalars) + [VMEM] * len(arrays),
        out_specs=[VMEM] * len(outs),
        scratch_shapes=[pltpu.VMEM(shape, f32) for shape in scratch],
        compiler_params=pltpu.CompilerParams(vmem_limit_bytes=mib * MIB),
        cost_estimate=pl.CostEstimate(flops=int(micros * 1.1e9), bytes_accessed=4096, transcendentals=0),
        name=name,
    )(*scalars, *arrays)


def flip(value, axis, mask):
    count = lax.axis_size(axis)
    return lax.ppermute(value, axis, [(i, i ^ mask) for i in range(count)])


def gather_first(value):
    middle = PIECE_ROWS // 2
    near, far = flip(value, "row", 2), flip(value, "row", 6)
    parts = [value, near, far, flip(near[:middle], "row", 6), flip(far[middle:], "row", 2)]
    pieces = []
    for part in parts:
        pieces += [part, flip(part, "row", 1)]
    return pieces


def wider(value, bit):
    return jnp.concatenate([value, flip(value, "leaf", 1 << bit)], axis=0)


def gather_row(value):
    return lax.all_gather(value, "row", axis=0, tiled=True)


def block_tables(maps, leaf):
    rows = []
    for level, one in ((1, maps[0]), (2, maps[1]), (3, maps[2])):
        child = leaf >> (level - 1)
        for front in (child, child ^ 1):
            rows.append(lax.dynamic_index_in_dim(one, front, 0, keepdims=True))
    blocks = jnp.concatenate(rows, axis=0)
    spots = jnp.arange(FRONT // BLOCK, dtype=jnp.int32)
    order = jnp.arange(UPD_BLOCKS, dtype=jnp.int32)
    hit = blocks[:, :, None] == spots
    place = jnp.sum(jnp.where(hit, order[:, None] + 1, 0), axis=1) - 1
    before = jnp.sum((blocks[:, :, None] < spots).astype(jnp.int32), axis=1)
    rank = jnp.where(place >= 0, before, -1)
    smaller = jnp.sum((blocks[:, :, None] > blocks[:, None, :]).astype(jnp.int32), axis=2)
    by_rank = jnp.sum(jnp.where(smaller[:, :, None] == order, order[:, None], 0), axis=1)
    return jnp.concatenate([place, rank, by_rank], axis=1).astype(jnp.int32).reshape(-1)


def body(panel0, panel1, panel2, panel3, maps1, maps2, maps3):
    panels = (panel0, panel1, panel2, panel3)
    leaf = lax.axis_index("leaf")
    row = lax.axis_index("row")
    tables = block_tables((maps1, maps2, maps3), leaf)
    places = [jnp.stack([row // 2, row % 2, leaf % (1 << level)]).astype(jnp.int32) for level in range(4)]

    pieces = gather_first(panels[0])
    leaf1, leaf2, leaf3 = [wider(panels[level], 0) for level in (1, 2, 3)]
    *pieces, leaf1, leaf2, leaf3 = lax.optimization_barrier((*pieces, leaf1, leaf2, leaf3))
    gathered = {1: gather_row(leaf1)}
    flipped2, flipped3 = flip(leaf2, "leaf", 2), flip(leaf3, "leaf", 2)

    lead_shape, half_shape = (2 * HALF_ROWS, BLOCK), (HALF_ROWS, BLOCK)
    full_shape, share_shape = (UPD_BLOCKS * UPD, BLOCK), (SHARE_ROWS, BLOCK)
    rest_shape = (2 * SHARE_ROWS, BLOCK)
    pivot, below = call(
        first_place_kernel, "place0", [places[0]], pieces, [(PIV, PIV), (UPD, PIV)], [(FRONT, PIV)], 1, 16,
    )
    inverse = call(first_factor_kernel, "factor0", [], [pivot], [(PIV, PIV)], [], 18, 16)[0]
    inverse, flipped2, flipped3 = lax.optimization_barrier((inverse, flipped2, flipped3))
    weighted, parent, half = call(
        first_columns_kernel, "columns0", [places[0], tables], [inverse, below],
        [(UPD, PIV), lead_shape, half_shape], [], 5, 16,
    )
    update, share = call(
        first_update_kernel, "update0", [places[0], tables], [below, weighted],
        [full_shape, share_shape], [], 5, 20,
    )
    leaf3 = jnp.concatenate([leaf3, flipped3], axis=0)
    flipped3 = flip(leaf3, "leaf", 4)
    gathered[2] = gather_row(jnp.concatenate([leaf2, flipped2], axis=0))
    for level in (1, 2, 3):
        bit = 1 << (level - 1)
        same_share = flip(share, "leaf", bit)
        same, panel, _ = lax.optimization_barrier((flip(half, "leaf", bit), gathered[level], share))
        other = flip(same, "row", 1)
        pivot, below = call(
            functools.partial(place_kernel, level), f"place{level}", [places[level]], [panel],
            [(PIV, PIV), (UPD, PIV)], [(FRONT, PIV)], 2, 16,
        )
        inverse = call(
            functools.partial(factor_kernel, level), f"factor{level}", [places[level], tables],
            [pivot, parent, same, other], [(PIV, PIV)], [lead_shape], 18, 16,
        )[0]
        if level == 1:
            same_share, inverse, flipped3 = lax.optimization_barrier((same_share, inverse, flipped3))
            gathered[3] = gather_row(jnp.concatenate([leaf3, flipped3], axis=0))
        else:
            same_share, inverse = lax.optimization_barrier((same_share, inverse))
        other_share = flip(same_share, "row", 1)
        operands = [inverse, below, update, same, other, same_share, other_share]
        if level == 3:
            return call(
                functools.partial(last_kernel, level), "last", [places[level], tables], operands,
                [(UPD // 64, UPD)], [lead_shape, rest_shape, full_shape, (UPD, PIV)], 5, 26,
            )[0]
        columns, weighted, parent, half, trailing = call(
            functools.partial(columns_kernel, level), f"columns{level}", [places[level], tables], operands,
            [(UPD, PIV), (UPD, PIV), lead_shape, half_shape, full_shape],
            [lead_shape, rest_shape, full_shape], 8, 32,
        )
        update, share = call(
            functools.partial(update_body, level), f"update{level}", [places[level], tables],
            [columns, weighted, trailing], [full_shape, share_shape], [], 5, 24,
        )


def solution(mesh):
    panel = P(("leaf", "row"), None)
    return jax.shard_map(
        body, mesh=mesh, in_specs=(panel,) * 4 + (P(),) * 3, out_specs=panel, check_vma=False
    )
```

```python
import functools

import jax
import jax.numpy as jnp
from jax import lax
from jax.experimental import pallas as pl
from jax.experimental.pallas import tpu as pltpu
from jax.sharding import PartitionSpec as P

BLOCK = 128
PIV = 512
UPD = 1024
FRONT = PIV + UPD
SUB = 8
WIDTH = 16
PIV_BLOCKS = PIV // BLOCK
UPD_BLOCKS = UPD // BLOCK
PIECE_ROWS = 192
LOWER = [(p, q) for p in range(PIV_BLOCKS) for q in range(p + 1)]
REST = [(a, b) for a in range(PIV_BLOCKS, UPD_BLOCKS) for b in range(a + 1)]
HALF_ROWS = len(LOWER) * BLOCK // 2
SHARE_ROWS = len(REST) * BLOCK // 2
TABLE = 32
RANK = 12
ORDER = 24
MIB = 1024 * 1024

f32 = jnp.float32
bf16 = jnp.bfloat16


def split(x):
    high = x.astype(bf16)
    return high, (x - high.astype(f32)).astype(bf16)


def dot3(left, right, transposed=False):
    dims = (((1,), (1 if transposed else 0,)), ((), ()))
    dot = functools.partial(lax.dot_general, dimension_numbers=dims, preferred_element_type=f32)
    return dot(left[0], right[0]) + (dot(left[0], right[1]) + dot(left[1], right[0]))


def reciprocal(x):
    return 1.0 / x


def inverse_block(rows):
    count = len(rows)
    parts = WIDTH // SUB
    shape = (SUB, BLOCK)
    lane = lax.broadcasted_iota(jnp.int32, shape, 1)
    sub = lax.broadcasted_iota(jnp.int32, shape, 0)
    rows = list(rows)

    def row_of(x, t):
        return jnp.broadcast_to(x[t : t + 1, :], shape)

    def lane_of(x, l):
        return jnp.broadcast_to(x[:, l : l + 1], shape)

    for g in range(count // parts):
        base = g * WIDTH
        inside = (lane >= base) & (lane < base + WIDTH)
        cols = [[lane_of(rows[parts * g + h], base + i) for i in range(WIDTH)] for h in range(parts)]
        strip = [
            jnp.where(inside, jnp.where(lane == base + h * SUB + sub, 1.0, 0.0), rows[parts * g + h])
            for h in range(parts)
        ]
        for i in range(0, WIDTH, 2):
            h, t = i // SUB, i % SUB
            a, b = row_of(cols[h][i], t), row_of(cols[h][i + 1], t)
            c, d = row_of(cols[h][i], t + 1), row_of(cols[h][i + 1], t + 1)
            r = reciprocal(a * d - b * c)
            ar, br, cr, dr = a * r, b * r, c * r, d * r

            def eliminate(col):
                x, y = row_of(col[h], t), row_of(col[h], t + 1)
                f, e = dr * x - br * y, ar * y - cr * x
                out = [col[k] - (cols[k][i] * f + cols[k][i + 1] * e) for k in range(parts)]
                out[h] = jnp.where(sub == t, f, jnp.where(sub == t + 1, e, out[h]))
                return out

            for j in range(i + 2, WIDTH):
                done = eliminate([cols[k][j] for k in range(parts)])
                for k in range(parts):
                    cols[k][j] = done[k]
            strip = eliminate(strip)
        near = [v for v in range(parts * (g + 1), parts * (g + 2)) if v < count]
        far = [v for v in range(count) if v not in near and v // parts != g]
        wide = [row_of(strip[i // SUB], i % SUB) for i in range(WIDTH)] if near else []
        for v in near:
            terms = [lane_of(rows[v], base + i) * wide[i] for i in range(WIDTH)]
            while len(terms) > 1:
                terms = [terms[k] + terms[k + 1] for k in range(0, len(terms), 2)]
            rows[v] = jnp.where(inside, 0.0, rows[v]) - terms[0]
        above = [jnp.zeros((base, BLOCK), f32)] if base else []
        below = [jnp.zeros((BLOCK - base - WIDTH, BLOCK), f32)] if base + WIDTH < BLOCK else []
        padded = jnp.concatenate(above + strip + below, 0)
        update = dot3(split(jnp.concatenate([rows[v] for v in far], 0)), split(padded))
        for k, v in enumerate(far):
            rows[v] = jnp.where(inside, 0.0, rows[v]) - update[k * SUB : (k + 1) * SUB]
        for h in range(parts):
            rows[parts * g + h] = strip[h]
    return jnp.concatenate(rows, 0)


def invert(ref):
    for j in range(PIV_BLOCKS):
        js = slice(j * BLOCK, (j + 1) * BLOCK)
        inverse = inverse_block(
            [ref[j * BLOCK + v * SUB : j * BLOCK + (v + 1) * SUB, js] for v in range(BLOCK // SUB)]
        )
        others = list(range(j + 1, PIV_BLOCKS)) + list(range(j))
        inverse_s = split(inverse)
        left = {i: split(ref[i * BLOCK : (i + 1) * BLOCK, js]) for i in others}
        top = {k: dot3(inverse_s, split(ref[js, k * BLOCK : (k + 1) * BLOCK])) for k in others}
        top_s = {k: split(top[k]) for k in others}
        for i in others:
            rows = slice(i * BLOCK, (i + 1) * BLOCK)
            for k in others:
                columns = slice(k * BLOCK, (k + 1) * BLOCK)
                ref[rows, columns] = ref[rows, columns] - dot3(left[i], top_s[k])
            ref[rows, js] = -dot3(left[i], inverse_s)
        for k in others:
            ref[js, k * BLOCK : (k + 1) * BLOCK] = top[k]
        ref[js, js] = inverse


def rows_at(index, count):
    return pl.ds(pl.multiple_of(index * count, SUB), count)


def place_kernel(level, place, gathered, pivot, below, whole):
    count = PIECE_ROWS >> level
    for row in range(8):
        for t in range(1 << level):
            owner = (place[2] ^ t) * 8 + row
            start = row * PIECE_ROWS + t * count
            whole[rows_at(owner, count), :] = gathered[start : start + count, :]
    pivot[...] = whole[:PIV, :]
    below[...] = whole[PIV:, :]


def first_place_kernel(place, *refs):
    pieces, (pivot, below), (whole,) = refs[:10], refs[10:12], refs[12:]
    half = PIECE_ROWS // 2
    for k, first, count, spot in ((0, 0, 2, 0), (1, 0, 2, 1), (3, 0, 2, 2), (2, 0, 1, 3), (2, 1, 1, 4)):
        for c in range(2):
            owner = ((place[0] ^ k) * 2 + (place[1] ^ c)) * 2 + first
            rows = pl.ds(pl.multiple_of(owner * half, SUB), count * half)
            whole[rows, :] = pieces[spot * 2 + c][...]
    pivot[...] = whole[:PIV, :]
    below[...] = whole[PIV:, :]


def first_factor_kernel(pivot, inverse):
    inverse[...] = pivot[...]
    invert(inverse)


def join(place, same, other, both):
    count = same.shape[0]
    both[rows_at(place[1], count), :] = same[...]
    both[rows_at(1 - place[1], count), :] = other[...]


def leading(ref, i, j):
    i0, j0 = jnp.maximum(i, 0), jnp.maximum(j, 0)
    spot = lax.shift_right_logical(i0 * (i0 + 1), 1) + j0
    return jnp.where((i >= 0) & (j >= 0), ref[rows_at(spot, BLOCK), :], 0.0)


def factor_kernel(level, place, tables, pivot, mine, same, other, inverse, theirs):
    join(place, same, other, theirs)
    own = (level - 1) * 2 * TABLE + RANK
    for p, q in LOWER:
        ps, qs = slice(p * BLOCK, (p + 1) * BLOCK), slice(q * BLOCK, (q + 1) * BLOCK)
        added = leading(mine, tables[own + p], tables[own + q])
        added = added + leading(theirs, tables[own + TABLE + p], tables[own + TABLE + q])
        total = pivot[ps, qs] + added
        inverse[ps, qs] = total
        if p != q:
            inverse[qs, ps] = total.T
    invert(inverse)


def block_of(ref, index_a, index_b):
    present = (index_a >= 0) & (index_b >= 0)
    spot = jnp.maximum(index_a, 0) * UPD_BLOCKS + jnp.maximum(index_b, 0)
    return jnp.where(present, ref[rows_at(spot, BLOCK), :], 0.0)


def extended(tables, level, mine, theirs, p, q):
    own = (level - 1) * 2 * TABLE
    other = own + TABLE + RANK
    return block_of(mine, tables[own + p], tables[own + q]) + block_of(
        theirs, tables[other + p], tables[other + q]
    )


def mirror(place, lead_same, lead_other, rest_same, rest_other, lead, rest, theirs):
    join(place, lead_same, lead_other, lead)
    join(place, rest_same, rest_other, rest)
    for pairs, ref in ((LOWER, lead), (REST, rest)):
        for n, (a, b) in enumerate(pairs):
            block = ref[n * BLOCK : (n + 1) * BLOCK, :]
            spot = (a * UPD_BLOCKS + b) * BLOCK
            theirs[spot : spot + BLOCK, :] = block
            if a != b:
                spot = (b * UPD_BLOCKS + a) * BLOCK
                theirs[spot : spot + BLOCK, :] = block.T


def assemble_below(level, tables, below, mine, theirs, columns):
    for u in range(UPD_BLOCKS):
        us = slice(u * BLOCK, (u + 1) * BLOCK)
        for q in range(PIV_BLOCKS):
            qs = slice(q * BLOCK, (q + 1) * BLOCK)
            columns[us, qs] = below[us, qs] + extended(tables, level, mine, theirs, PIV_BLOCKS + u, q)


def lead_blocks(level, place, tables, trailing, columns, weighted, lead, half):
    order = level * 2 * TABLE + ORDER
    for n, (i, j) in enumerate(LOWER):
        a, b = tables[order + i], tables[order + j]
        block = -dot3(
            split(weighted[rows_at(a, BLOCK), :]), split(columns[rows_at(b, BLOCK), :]), transposed=True
        )
        if level:
            block = block + trailing[rows_at(a * UPD_BLOCKS + b, BLOCK), :]
        lead[n * BLOCK : (n + 1) * BLOCK, :] = block
    half[...] = lead[rows_at(place[1], HALF_ROWS), :]


def weigh(columns, inverse, weighted):
    inverse_s = split(inverse[...])
    for u in range(0, UPD, 256):
        weighted[u : u + 256, :] = dot3(split(columns[u : u + 256, :]), inverse_s)


def first_columns_kernel(place, tables, inverse, below, weighted, parent, half):
    weigh(below, inverse, weighted)
    lead_blocks(0, place, tables, None, below, weighted, parent, half)


def columns_kernel(
    level, place, tables, inverse, below, mine, lead_same, lead_other, rest_same, rest_other,
    columns, weighted, parent, half, trailing, lead, rest, theirs,
):
    mirror(place, lead_same, lead_other, rest_same, rest_other, lead, rest, theirs)
    assemble_below(level, tables, below, mine, theirs, columns)
    weigh(columns, inverse, weighted)
    for a in range(UPD_BLOCKS):
        for b in range(UPD_BLOCKS):
            spot = (a * UPD_BLOCKS + b) * BLOCK
            trailing[spot : spot + BLOCK, :] = extended(
                tables, level, mine, theirs, PIV_BLOCKS + a, PIV_BLOCKS + b
            )
    lead_blocks(level, place, tables, trailing, columns, weighted, parent, half)


def update_body(level, place, tables, columns, weighted, trailing, update, share):
    left = split(weighted[...])
    step = 2 * BLOCK
    for start in range(0, UPD, step):
        strip = dot3(left, split(columns[start : start + step, :]), transposed=True)
        for a in range(UPD_BLOCKS):
            for inner in range(2):
                b = start // BLOCK + inner
                spot = (a * UPD_BLOCKS + b) * BLOCK
                block = -strip[a * BLOCK : (a + 1) * BLOCK, inner * BLOCK : (inner + 1) * BLOCK]
                if trailing is not None:
                    block = trailing[spot : spot + BLOCK, :] + block
                update[spot : spot + BLOCK, :] = block
    order = level * 2 * TABLE + ORDER
    count = len(REST) // 2
    for n in range(count):
        (i0, j0), (i1, j1) = REST[n], REST[count + n]
        a = tables[order + i0 + place[1] * (i1 - i0)]
        b = tables[order + j0 + place[1] * (j1 - j0)]
        share[n * BLOCK : (n + 1) * BLOCK, :] = update[rows_at(a * UPD_BLOCKS + b, BLOCK), :]


def first_update_kernel(place, tables, columns, weighted, update, share):
    update_body(0, place, tables, columns, weighted, None, update, share)


def last_kernel(
    level, place, tables, inverse, below, mine, lead_same, lead_other, rest_same, rest_other,
    out, lead, rest, theirs, columns,
):
    mirror(place, lead_same, lead_other, rest_same, rest_other, lead, rest, theirs)
    assemble_below(level, tables, below, mine, theirs, columns)
    count = out.shape[0]
    position = place[2] * 8 + place[0] * 2 + place[1]
    per_block = BLOCK // count
    block_row, inner = position // per_block, position % per_block
    left = split(columns[rows_at(position, count), :])
    weighted = split(dot3(left, split(inverse[...])))
    strip = dot3(weighted, split(columns[...]), transposed=True)
    own = (level - 1) * 2 * TABLE
    sibling = own + TABLE + RANK

    def part(ref, index_a, index_b):
        present = (index_a >= 0) & (index_b >= 0)
        spot = (jnp.maximum(index_a, 0) * UPD_BLOCKS + jnp.maximum(index_b, 0)) * per_block + inner
        return jnp.where(present, ref[rows_at(spot, count), :], 0.0)

    for v in range(UPD_BLOCKS):
        mine_a, mine_b = tables[own + PIV_BLOCKS + block_row], tables[own + PIV_BLOCKS + v]
        their_a, their_b = tables[sibling + PIV_BLOCKS + block_row], tables[sibling + PIV_BLOCKS + v]
        vs = slice(v * BLOCK, (v + 1) * BLOCK)
        out[:, vs] = part(mine, mine_a, mine_b) + part(theirs, their_a, their_b) - strip[:, vs]


SMEM = pl.BlockSpec(memory_space=pltpu.SMEM)
VMEM = pl.BlockSpec(memory_space=pltpu.VMEM)


def call(kernel, name, scalars, arrays, outs, scratch, micros, mib):
    shapes = [jax.ShapeDtypeStruct(shape, f32) for shape in outs]
    return pl.pallas_call(
        kernel,
        out_shape=shapes,
        in_specs=[SMEM] * len(scalars) + [VMEM] * len(arrays),
        out_specs=[VMEM] * len(outs),
        scratch_shapes=[pltpu.VMEM(shape, f32) for shape in scratch],
        compiler_params=pltpu.CompilerParams(vmem_limit_bytes=mib * MIB),
        cost_estimate=pl.CostEstimate(flops=int(micros * 1.1e9), bytes_accessed=4096, transcendentals=0),
        name=name,
    )(*scalars, *arrays)


def flip(value, axis, mask):
    count = lax.axis_size(axis)
    return lax.ppermute(value, axis, [(i, i ^ mask) for i in range(count)])


def gather_first(value):
    middle = PIECE_ROWS // 2
    near, far = flip(value, "row", 2), flip(value, "row", 6)
    parts = [value, near, far, flip(near[:middle], "row", 6), flip(far[middle:], "row", 2)]
    pieces = []
    for part in parts:
        pieces += [part, flip(part, "row", 1)]
    return pieces


def wider(value, bit):
    return jnp.concatenate([value, flip(value, "leaf", 1 << bit)], axis=0)


def gather_row(value):
    return lax.all_gather(value, "row", axis=0, tiled=True)


def block_tables(maps, leaf):
    rows = []
    for level, one in ((1, maps[0]), (2, maps[1]), (3, maps[2])):
        child = leaf >> (level - 1)
        for front in (child, child ^ 1):
            rows.append(lax.dynamic_index_in_dim(one, front, 0, keepdims=True))
    blocks = jnp.concatenate(rows, axis=0)
    spots = jnp.arange(FRONT // BLOCK, dtype=jnp.int32)
    order = jnp.arange(UPD_BLOCKS, dtype=jnp.int32)
    hit = blocks[:, :, None] == spots
    place = jnp.sum(jnp.where(hit, order[:, None] + 1, 0), axis=1) - 1
    before = jnp.sum((blocks[:, :, None] < spots).astype(jnp.int32), axis=1)
    rank = jnp.where(place >= 0, before, -1)
    smaller = jnp.sum((blocks[:, :, None] > blocks[:, None, :]).astype(jnp.int32), axis=2)
    by_rank = jnp.sum(jnp.where(smaller[:, :, None] == order, order[:, None], 0), axis=1)
    return jnp.concatenate([place, rank, by_rank], axis=1).astype(jnp.int32).reshape(-1)


def body(panel0, panel1, panel2, panel3, maps1, maps2, maps3):
    panels = (panel0, panel1, panel2, panel3)
    leaf = lax.axis_index("leaf")
    row = lax.axis_index("row")
    tables = block_tables((maps1, maps2, maps3), leaf)
    places = [jnp.stack([row // 2, row % 2, leaf % (1 << level)]).astype(jnp.int32) for level in range(4)]

    pieces = gather_first(panels[0])
    leaf1, leaf2, leaf3 = [wider(panels[level], 0) for level in (1, 2, 3)]
    *pieces, leaf1, leaf2, leaf3, tables = lax.optimization_barrier((*pieces, leaf1, leaf2, leaf3, tables))
    gathered = {1: gather_row(leaf1)}
    flipped2, flipped3 = flip(leaf2, "leaf", 2), flip(leaf3, "leaf", 2)

    lead_shape, half_shape = (2 * HALF_ROWS, BLOCK), (HALF_ROWS, BLOCK)
    full_shape, share_shape = (UPD_BLOCKS * UPD, BLOCK), (SHARE_ROWS, BLOCK)
    rest_shape = (2 * SHARE_ROWS, BLOCK)
    pivot, below = call(
        first_place_kernel, "place0", [places[0]], pieces, [(PIV, PIV), (UPD, PIV)], [(FRONT, PIV)], 1, 16,
    )
    inverse = call(first_factor_kernel, "factor0", [], [pivot], [(PIV, PIV)], [], 18, 16)[0]
    inverse, flipped2, flipped3 = lax.optimization_barrier((inverse, flipped2, flipped3))
    weighted, parent, half = call(
        first_columns_kernel, "columns0", [places[0], tables], [inverse, below],
        [(UPD, PIV), lead_shape, half_shape], [], 5, 16,
    )
    update, share = call(
        first_update_kernel, "update0", [places[0], tables], [below, weighted],
        [full_shape, share_shape], [], 5, 20,
    )
    leaf3 = jnp.concatenate([leaf3, flipped3], axis=0)
    flipped3 = flip(leaf3, "leaf", 4)
    gathered[2] = gather_row(jnp.concatenate([leaf2, flipped2], axis=0))
    for level in (1, 2, 3):
        bit = 1 << (level - 1)
        same_share = flip(share, "leaf", bit)
        if level == 1:
            same, panel, _ = lax.optimization_barrier((flip(half, "leaf", bit), gathered[1], share))
        else:
            same, _ = lax.optimization_barrier((flip(half, "leaf", bit), share))
        other = flip(same, "row", 1)
        pivot, below = call(
            functools.partial(place_kernel, level), f"place{level}", [places[level]], [panel],
            [(PIV, PIV), (UPD, PIV)], [(FRONT, PIV)], 2, 16,
        )
        inverse = call(
            functools.partial(factor_kernel, level), f"factor{level}", [places[level], tables],
            [pivot, parent, same, other], [(PIV, PIV)], [lead_shape], 6, 16,
        )[0]
        if level == 1:
            same_share, inverse, flipped3, panel = lax.optimization_barrier(
                (same_share, inverse, flipped3, gathered[2])
            )
            gathered[3] = gather_row(jnp.concatenate([leaf3, flipped3], axis=0))
        elif level == 2:
            same_share, inverse, panel = lax.optimization_barrier((same_share, inverse, gathered[3]))
        else:
            same_share, inverse = lax.optimization_barrier((same_share, inverse))
        other_share = flip(same_share, "row", 1)
        operands = [inverse, below, update, same, other, same_share, other_share]
        if level == 3:
            return call(
                functools.partial(last_kernel, level), "last", [places[level], tables], operands,
                [(UPD // 64, UPD)], [lead_shape, rest_shape, full_shape, (UPD, PIV)], 5, 26,
            )[0]
        columns, weighted, parent, half, trailing = call(
            functools.partial(columns_kernel, level), f"columns{level}", [places[level], tables], operands,
            [(UPD, PIV), (UPD, PIV), lead_shape, half_shape, full_shape],
            [lead_shape, rest_shape, full_shape], 8, 32,
        )
        update, share = call(
            functools.partial(update_body, level), f"update{level}", [places[level], tables],
            [columns, weighted, trailing], [full_shape, share_shape], [], 5, 24,
        )


def solution(mesh):
    panel = P(("leaf", "row"), None)
    return jax.shard_map(
        body, mesh=mesh, in_specs=(panel,) * 4 + (P(),) * 3, out_specs=panel, check_vma=False
    )
```

```python
import functools

import jax
import jax.numpy as jnp
from jax import lax
from jax.experimental import pallas as pl
from jax.experimental.pallas import tpu as pltpu
from jax.sharding import PartitionSpec as P

BLOCK = 128
PIV = 512
UPD = 1024
FRONT = PIV + UPD
SUB = 8
WIDTH = 16
PIV_BLOCKS = PIV // BLOCK
UPD_BLOCKS = UPD // BLOCK
PIECE_ROWS = 192
LOWER = [(p, q) for p in range(PIV_BLOCKS) for q in range(p + 1)]
REST = [(a, b) for a in range(PIV_BLOCKS, UPD_BLOCKS) for b in range(a + 1)]
HALF_ROWS = len(LOWER) * BLOCK // 2
SHARE_ROWS = len(REST) * BLOCK // 2
TABLE = 32
RANK = 12
ORDER = 24
MIB = 1024 * 1024

f32 = jnp.float32
bf16 = jnp.bfloat16


def split(x):
    high = x.astype(bf16)
    return high, (x - high.astype(f32)).astype(bf16)


def dot3(left, right, transposed=False):
    dims = (((1,), (1 if transposed else 0,)), ((), ()))
    dot = functools.partial(lax.dot_general, dimension_numbers=dims, preferred_element_type=f32)
    return dot(left[0], right[0]) + (dot(left[0], right[1]) + dot(left[1], right[0]))


def reciprocal(x):
    return 1.0 / x


def inverse_block(rows):
    count = len(rows)
    parts = WIDTH // SUB
    shape = (SUB, BLOCK)
    lane = lax.broadcasted_iota(jnp.int32, shape, 1)
    sub = lax.broadcasted_iota(jnp.int32, shape, 0)
    rows = list(rows)

    def row_of(x, t):
        return jnp.broadcast_to(x[t : t + 1, :], shape)

    def lane_of(x, l):
        return jnp.broadcast_to(x[:, l : l + 1], shape)

    for g in range(count // parts):
        base = g * WIDTH
        inside = (lane >= base) & (lane < base + WIDTH)
        cols = [[lane_of(rows[parts * g + h], base + i) for i in range(WIDTH)] for h in range(parts)]
        strip = [
            jnp.where(inside, jnp.where(lane == base + h * SUB + sub, 1.0, 0.0), rows[parts * g + h])
            for h in range(parts)
        ]
        for i in range(0, WIDTH, 2):
            h, t = i // SUB, i % SUB
            a, b = row_of(cols[h][i], t), row_of(cols[h][i + 1], t)
            c, d = row_of(cols[h][i], t + 1), row_of(cols[h][i + 1], t + 1)
            r = reciprocal(a * d - b * c)
            ar, br, cr, dr = a * r, b * r, c * r, d * r

            def eliminate(col):
                x, y = row_of(col[h], t), row_of(col[h], t + 1)
                f, e = dr * x - br * y, ar * y - cr * x
                out = [col[k] - (cols[k][i] * f + cols[k][i + 1] * e) for k in range(parts)]
                out[h] = jnp.where(sub == t, f, jnp.where(sub == t + 1, e, out[h]))
                return out

            for j in range(i + 2, WIDTH):
                done = eliminate([cols[k][j] for k in range(parts)])
                for k in range(parts):
                    cols[k][j] = done[k]
            strip = eliminate(strip)
        near = [v for v in range(parts * (g + 1), parts * (g + 2)) if v < count]
        far = [v for v in range(count) if v not in near and v // parts != g]
        wide = [row_of(strip[i // SUB], i % SUB) for i in range(WIDTH)] if near else []
        for v in near:
            terms = [lane_of(rows[v], base + i) * wide[i] for i in range(WIDTH)]
            while len(terms) > 1:
                terms = [terms[k] + terms[k + 1] for k in range(0, len(terms), 2)]
            rows[v] = jnp.where(inside, 0.0, rows[v]) - terms[0]
        above = [jnp.zeros((base, BLOCK), f32)] if base else []
        below = [jnp.zeros((BLOCK - base - WIDTH, BLOCK), f32)] if base + WIDTH < BLOCK else []
        padded = jnp.concatenate(above + strip + below, 0)
        update = dot3(split(jnp.concatenate([rows[v] for v in far], 0)), split(padded))
        for k, v in enumerate(far):
            rows[v] = jnp.where(inside, 0.0, rows[v]) - update[k * SUB : (k + 1) * SUB]
        for h in range(parts):
            rows[parts * g + h] = strip[h]
    return jnp.concatenate(rows, 0)


def invert(ref):
    for j in range(PIV_BLOCKS):
        js = slice(j * BLOCK, (j + 1) * BLOCK)
        inverse = inverse_block(
            [ref[j * BLOCK + v * SUB : j * BLOCK + (v + 1) * SUB, js] for v in range(BLOCK // SUB)]
        )
        others = list(range(j + 1, PIV_BLOCKS)) + list(range(j))
        inverse_s = split(inverse)
        left = {i: split(ref[i * BLOCK : (i + 1) * BLOCK, js]) for i in others}
        top = {k: dot3(inverse_s, split(ref[js, k * BLOCK : (k + 1) * BLOCK])) for k in others}
        top_s = {k: split(top[k]) for k in others}
        for i in others:
            rows = slice(i * BLOCK, (i + 1) * BLOCK)
            for k in others:
                columns = slice(k * BLOCK, (k + 1) * BLOCK)
                ref[rows, columns] = ref[rows, columns] - dot3(left[i], top_s[k])
            ref[rows, js] = -dot3(left[i], inverse_s)
        for k in others:
            ref[js, k * BLOCK : (k + 1) * BLOCK] = top[k]
        ref[js, js] = inverse


def rows_at(index, count):
    return pl.ds(pl.multiple_of(index * count, SUB), count)


def place_kernel(level, place, gathered, pivot, below, whole):
    count = PIECE_ROWS >> level
    for row in range(8):
        for t in range(1 << level):
            owner = (place[2] ^ t) * 8 + row
            start = row * PIECE_ROWS + t * count
            whole[rows_at(owner, count), :] = gathered[start : start + count, :]
    pivot[...] = whole[:PIV, :]
    below[...] = whole[PIV:, :]


def first_place_kernel(place, *refs):
    pieces, (pivot, below), (whole,) = refs[:10], refs[10:12], refs[12:]
    half = PIECE_ROWS // 2
    for k, first, count, spot in ((0, 0, 2, 0), (1, 0, 2, 1), (3, 0, 2, 2), (2, 0, 1, 3), (2, 1, 1, 4)):
        for c in range(2):
            owner = ((place[0] ^ k) * 2 + (place[1] ^ c)) * 2 + first
            rows = pl.ds(pl.multiple_of(owner * half, SUB), count * half)
            whole[rows, :] = pieces[spot * 2 + c][...]
    pivot[...] = whole[:PIV, :]
    below[...] = whole[PIV:, :]


def first_factor_kernel(pivot, inverse):
    inverse[...] = pivot[...]
    invert(inverse)


def join(place, same, other, both):
    count = same.shape[0]
    both[rows_at(place[1], count), :] = same[...]
    both[rows_at(1 - place[1], count), :] = other[...]


def leading(ref, i, j):
    i0, j0 = jnp.maximum(i, 0), jnp.maximum(j, 0)
    spot = lax.shift_right_logical(i0 * (i0 + 1), 1) + j0
    return jnp.where((i >= 0) & (j >= 0), ref[rows_at(spot, BLOCK), :], 0.0)


def factor_kernel(level, place, tables, pivot, mine, same, other, inverse, theirs):
    join(place, same, other, theirs)
    own = (level - 1) * 2 * TABLE + RANK
    for p, q in LOWER:
        ps, qs = slice(p * BLOCK, (p + 1) * BLOCK), slice(q * BLOCK, (q + 1) * BLOCK)
        added = leading(mine, tables[own + p], tables[own + q])
        added = added + leading(theirs, tables[own + TABLE + p], tables[own + TABLE + q])
        total = pivot[ps, qs] + added
        inverse[ps, qs] = total
        if p != q:
            inverse[qs, ps] = total.T
    invert(inverse)


def block_of(ref, index_a, index_b):
    present = (index_a >= 0) & (index_b >= 0)
    spot = jnp.maximum(index_a, 0) * UPD_BLOCKS + jnp.maximum(index_b, 0)
    return jnp.where(present, ref[rows_at(spot, BLOCK), :], 0.0)


def extended(tables, level, mine, theirs, p, q):
    own = (level - 1) * 2 * TABLE
    other = own + TABLE + RANK
    return block_of(mine, tables[own + p], tables[own + q]) + block_of(
        theirs, tables[other + p], tables[other + q]
    )


def mirror(place, lead_same, lead_other, rest_same, rest_other, lead, rest, theirs):
    join(place, lead_same, lead_other, lead)
    join(place, rest_same, rest_other, rest)
    for pairs, ref in ((LOWER, lead), (REST, rest)):
        for n, (a, b) in enumerate(pairs):
            block = ref[n * BLOCK : (n + 1) * BLOCK, :]
            spot = (a * UPD_BLOCKS + b) * BLOCK
            theirs[spot : spot + BLOCK, :] = block
            if a != b:
                spot = (b * UPD_BLOCKS + a) * BLOCK
                theirs[spot : spot + BLOCK, :] = block.T


def assemble_below(level, tables, below, mine, theirs, columns):
    for u in range(UPD_BLOCKS):
        us = slice(u * BLOCK, (u + 1) * BLOCK)
        for q in range(PIV_BLOCKS):
            qs = slice(q * BLOCK, (q + 1) * BLOCK)
            columns[us, qs] = below[us, qs] + extended(tables, level, mine, theirs, PIV_BLOCKS + u, q)


def lead_blocks(level, place, tables, trailing, columns, weighted, lead, half):
    order = level * 2 * TABLE + ORDER
    for n, (i, j) in enumerate(LOWER):
        a, b = tables[order + i], tables[order + j]
        block = -dot3(
            split(weighted[rows_at(a, BLOCK), :]), split(columns[rows_at(b, BLOCK), :]), transposed=True
        )
        if level:
            block = block + trailing[rows_at(a * UPD_BLOCKS + b, BLOCK), :]
        lead[n * BLOCK : (n + 1) * BLOCK, :] = block
    half[...] = lead[rows_at(place[1], HALF_ROWS), :]


def weigh(columns, inverse, weighted):
    inverse_s = split(inverse[...])
    for u in range(0, UPD, 256):
        weighted[u : u + 256, :] = dot3(split(columns[u : u + 256, :]), inverse_s)


def first_columns_kernel(place, tables, inverse, below, weighted, parent, half):
    weigh(below, inverse, weighted)
    lead_blocks(0, place, tables, None, below, weighted, parent, half)


def columns_kernel(
    level, place, tables, inverse, below, mine, lead_same, lead_other, rest_same, rest_other,
    columns, weighted, parent, half, trailing, lead, rest, theirs,
):
    mirror(place, lead_same, lead_other, rest_same, rest_other, lead, rest, theirs)
    assemble_below(level, tables, below, mine, theirs, columns)
    weigh(columns, inverse, weighted)
    for a in range(UPD_BLOCKS):
        for b in range(UPD_BLOCKS):
            spot = (a * UPD_BLOCKS + b) * BLOCK
            trailing[spot : spot + BLOCK, :] = extended(
                tables, level, mine, theirs, PIV_BLOCKS + a, PIV_BLOCKS + b
            )
    lead_blocks(level, place, tables, trailing, columns, weighted, parent, half)


def update_body(level, place, tables, columns, weighted, trailing, update, share):
    left = split(weighted[...])
    step = 2 * BLOCK
    for start in range(0, UPD, step):
        strip = dot3(left, split(columns[start : start + step, :]), transposed=True)
        for a in range(UPD_BLOCKS):
            for inner in range(2):
                b = start // BLOCK + inner
                spot = (a * UPD_BLOCKS + b) * BLOCK
                block = -strip[a * BLOCK : (a + 1) * BLOCK, inner * BLOCK : (inner + 1) * BLOCK]
                if trailing is not None:
                    block = trailing[spot : spot + BLOCK, :] + block
                update[spot : spot + BLOCK, :] = block
    order = level * 2 * TABLE + ORDER
    count = len(REST) // 2
    for n in range(count):
        (i0, j0), (i1, j1) = REST[n], REST[count + n]
        a = tables[order + i0 + place[1] * (i1 - i0)]
        b = tables[order + j0 + place[1] * (j1 - j0)]
        share[n * BLOCK : (n + 1) * BLOCK, :] = update[rows_at(a * UPD_BLOCKS + b, BLOCK), :]


def first_update_kernel(place, tables, columns, weighted, update, share):
    update_body(0, place, tables, columns, weighted, None, update, share)


def last_kernel(
    level, place, tables, inverse, below, mine, lead_same, lead_other, rest_same, rest_other,
    out, lead, rest, theirs, columns,
):
    mirror(place, lead_same, lead_other, rest_same, rest_other, lead, rest, theirs)
    assemble_below(level, tables, below, mine, theirs, columns)
    count = out.shape[0]
    position = place[2] * 8 + place[0] * 2 + place[1]
    per_block = BLOCK // count
    block_row, inner = position // per_block, position % per_block
    left = split(columns[rows_at(position, count), :])
    weighted = split(dot3(left, split(inverse[...])))
    strip = dot3(weighted, split(columns[...]), transposed=True)
    own = (level - 1) * 2 * TABLE
    sibling = own + TABLE + RANK

    def part(ref, index_a, index_b):
        present = (index_a >= 0) & (index_b >= 0)
        spot = (jnp.maximum(index_a, 0) * UPD_BLOCKS + jnp.maximum(index_b, 0)) * per_block + inner
        return jnp.where(present, ref[rows_at(spot, count), :], 0.0)

    for v in range(UPD_BLOCKS):
        mine_a, mine_b = tables[own + PIV_BLOCKS + block_row], tables[own + PIV_BLOCKS + v]
        their_a, their_b = tables[sibling + PIV_BLOCKS + block_row], tables[sibling + PIV_BLOCKS + v]
        vs = slice(v * BLOCK, (v + 1) * BLOCK)
        out[:, vs] = part(mine, mine_a, mine_b) + part(theirs, their_a, their_b) - strip[:, vs]


SMEM = pl.BlockSpec(memory_space=pltpu.SMEM)
VMEM = pl.BlockSpec(memory_space=pltpu.VMEM)


def call(kernel, name, scalars, arrays, outs, scratch, micros, mib):
    shapes = [jax.ShapeDtypeStruct(shape, f32) for shape in outs]
    return pl.pallas_call(
        kernel,
        out_shape=shapes,
        in_specs=[SMEM] * len(scalars) + [VMEM] * len(arrays),
        out_specs=[VMEM] * len(outs),
        scratch_shapes=[pltpu.VMEM(shape, f32) for shape in scratch],
        compiler_params=pltpu.CompilerParams(vmem_limit_bytes=mib * MIB),
        cost_estimate=pl.CostEstimate(flops=int(micros * 1.1e9), bytes_accessed=4096, transcendentals=0),
        name=name,
    )(*scalars, *arrays)


def flip(value, axis, mask):
    count = lax.axis_size(axis)
    return lax.ppermute(value, axis, [(i, i ^ mask) for i in range(count)])


def gather_first(value):
    middle = PIECE_ROWS // 2
    near, far = flip(value, "row", 2), flip(value, "row", 6)
    parts = [value, near, far, flip(near[:middle], "row", 6), flip(far[middle:], "row", 2)]
    pieces = []
    for part in parts:
        pieces += [part, flip(part, "row", 1)]
    return pieces


def wider(value, bit):
    return jnp.concatenate([value, flip(value, "leaf", 1 << bit)], axis=0)


def gather_row(value):
    return lax.all_gather(value, "row", axis=0, tiled=True)


def block_tables(maps, leaf):
    rows = []
    for level, one in ((1, maps[0]), (2, maps[1]), (3, maps[2])):
        child = leaf >> (level - 1)
        for front in (child, child ^ 1):
            rows.append(lax.dynamic_index_in_dim(one, front, 0, keepdims=True))
    blocks = jnp.concatenate(rows, axis=0)
    spots = jnp.arange(FRONT // BLOCK, dtype=jnp.int32)
    order = jnp.arange(UPD_BLOCKS, dtype=jnp.int32)
    hit = blocks[:, :, None] == spots
    place = jnp.sum(jnp.where(hit, order[:, None] + 1, 0), axis=1) - 1
    before = jnp.sum((blocks[:, :, None] < spots).astype(jnp.int32), axis=1)
    rank = jnp.where(place >= 0, before, -1)
    smaller = jnp.sum((blocks[:, :, None] > blocks[:, None, :]).astype(jnp.int32), axis=2)
    by_rank = jnp.sum(jnp.where(smaller[:, :, None] == order, order[:, None], 0), axis=1)
    return jnp.concatenate([place, rank, by_rank], axis=1).astype(jnp.int32).reshape(-1)


def body(panel0, panel1, panel2, panel3, maps1, maps2, maps3):
    panels = (panel0, panel1, panel2, panel3)
    leaf = lax.axis_index("leaf")
    row = lax.axis_index("row")
    tables = block_tables((maps1, maps2, maps3), leaf)
    places = [jnp.stack([row // 2, row % 2, leaf % (1 << level)]).astype(jnp.int32) for level in range(4)]

    pieces = gather_first(panels[0])
    leaf1, leaf2, leaf3 = [wider(panels[level], 0) for level in (1, 2, 3)]
    *pieces, leaf1, leaf2, leaf3, tables = lax.optimization_barrier((*pieces, leaf1, leaf2, leaf3, tables))
    gathered = {1: gather_row(leaf1)}
    flipped2, flipped3 = flip(leaf2, "leaf", 2), flip(leaf3, "leaf", 2)

    lead_shape, half_shape = (2 * HALF_ROWS, BLOCK), (HALF_ROWS, BLOCK)
    full_shape, share_shape = (UPD_BLOCKS * UPD, BLOCK), (SHARE_ROWS, BLOCK)
    rest_shape = (2 * SHARE_ROWS, BLOCK)
    pivot, below = call(
        first_place_kernel, "place0", [places[0]], pieces, [(PIV, PIV), (UPD, PIV)], [(FRONT, PIV)], 1, 16,
    )
    inverse = call(first_factor_kernel, "factor0", [], [pivot], [(PIV, PIV)], [], 18, 16)[0]
    weighted, parent, half = call(
        first_columns_kernel, "columns0", [places[0], tables], [inverse, below],
        [(UPD, PIV), lead_shape, half_shape], [], 5, 16,
    )
    weighted, half, flipped2, flipped3 = lax.optimization_barrier((weighted, half, flipped2, flipped3))
    update, share = call(
        first_update_kernel, "update0", [places[0], tables], [below, weighted],
        [full_shape, share_shape], [], 5, 20,
    )
    for level in (1, 2, 3):
        bit = 1 << (level - 1)
        same_share = flip(share, "leaf", bit)
        same, panel, _ = lax.optimization_barrier((flip(half, "leaf", bit), gathered[level], share))
        if level == 1:
            same, flipped2, flipped3 = lax.optimization_barrier((same, flipped2, flipped3))
            leaf3 = jnp.concatenate([leaf3, flipped3], axis=0)
            flipped3 = flip(leaf3, "leaf", 4)
            gathered[2] = gather_row(jnp.concatenate([leaf2, flipped2], axis=0))
        if level == 2:
            same, flipped3 = lax.optimization_barrier((same, flipped3))
            gathered[3] = gather_row(jnp.concatenate([leaf3, flipped3], axis=0))
        other = flip(same, "row", 1)
        pivot, below = call(
            functools.partial(place_kernel, level), f"place{level}", [places[level]], [panel],
            [(PIV, PIV), (UPD, PIV)], [(FRONT, PIV)], 2, 16,
        )
        inverse = call(
            functools.partial(factor_kernel, level), f"factor{level}", [places[level], tables],
            [pivot, parent, same, other], [(PIV, PIV)], [lead_shape], 18, 16,
        )[0]
        same_share, inverse = lax.optimization_barrier((same_share, inverse))
        other_share = flip(same_share, "row", 1)
        operands = [inverse, below, update, same, other, same_share, other_share]
        if level == 3:
            return call(
                functools.partial(last_kernel, level), "last", [places[level], tables], operands,
                [(UPD // 64, UPD)], [lead_shape, rest_shape, full_shape, (UPD, PIV)], 5, 26,
            )[0]
        columns, weighted, parent, half, trailing = call(
            functools.partial(columns_kernel, level), f"columns{level}", [places[level], tables], operands,
            [(UPD, PIV), (UPD, PIV), lead_shape, half_shape, full_shape],
            [lead_shape, rest_shape, full_shape], 8, 32,
        )
        if level == 1:
            weighted, half, flipped3 = lax.optimization_barrier((weighted, half, flipped3))
        update, share = call(
            functools.partial(update_body, level), f"update{level}", [places[level], tables],
            [columns, weighted, trailing], [full_shape, share_shape], [], 5, 24,
        )


def solution(mesh):
    panel = P(("leaf", "row"), None)
    return jax.shard_map(
        body, mesh=mesh, in_specs=(panel,) * 4 + (P(),) * 3, out_specs=panel, check_vma=False
    )
```
